256 devices in a mesh: region: 16 (over y, x), dp: 16 (over z, core).
Axes of the slice: x: 4, y: 4, z: 8, core: 2. Of those that a mesh axis runs over, the one named last changes fastest.
Arguments:
- positions: float32 [3, 4096, 128], P(None, ('region', 'dp')), may hold values from -1 to 1
- spacing: float32 [4096, 128], P(('region', 'dp')), may hold values from 0.015 to 0.15
- targets: float32 [3, 4096], P(None, ('region', 'dp')), may hold values from 0 to 1
- frequencies: float32 [3, 64], replicated, may hold values from -12 to 12
- seg_region: int32 [16384, 1], P(('region', 'dp')), may hold values from 0 to 15; in each aligned block of 64 rows (0 to 63, 64 to 127, ...) at most 8 rows name the same one
- w_in: bfloat16 [16, 128, 256], P('region'), may hold values from -0.5 to 0.5
- w_hidden: bfloat16 [16, 4, 256, 256], P('region'), may hold values from -0.375 to 0.375
- w_head: bfloat16 [16, 4, 256], P('region'), may hold values from -1 to 1
Outputs:
- pixel_color: float32 [3, 4096], P(None, ('region', 'dp'))
- grad_in: float32 [16, 128, 256], P('region', 'dp')
- grad_hidden: float32 [16, 4, 256, 256], P('region', None, 'dp')
- grad_head: float32 [16, 4, 256], P('region', None, 'dp')
The draws below stay inside these ranges and needn't reach their ends.
Inputs may be any that keep to these rules, and one draw needn't show every extreme that they name: `seg_region`: among the 64 segments of one device, no region is named more than 8 times, a bound that some block reaches.
All inputs are finite; a program needn't handle non-finite values.
Results may differ from the reference program's by a relative error of at most 0.034.
Values may be sent and summed in bfloat16 or wider, within the bound.
No kernel may reach another device: no remote copies, remote signals or barrier semaphores. Data moves between devices by JAX's collectives and lax.ppermute only.
A program may use at most 128 MiB of HBM per device.

```python
import math
import jax
import jax.numpy as jnp
import numpy as np
from jax import lax

SEG_LEN = 32
ENC = 128
HID = 256
LAYERS = 4
SAMPLES = 128
REGIONS = 16
RAYS = 4096
SEG_DEV = 64
SEGMENTS = 16384
CAP = 8


def level_of(own_key, dims, cuts, smallest, largest):
    def one(axis_at, shards_of):
        steps = jax.random.uniform(jax.random.fold_in(jax.random.fold_in(own_key, 6), axis_at), (shards_of,), jnp.float32, smallest / len(cuts), largest / len(cuts))
        return jnp.repeat(jnp.exp(steps), dims[axis_at] // shards_of).reshape((-1,) + (1,) * (len(dims) - axis_at - 1))

    level = one(*cuts[0])
    for cut in cuts[1:]:
        level = level * one(*cut)
    return level


def deal_out(stream_key, own, number, rows, number_of, top, limit, skew):
    sequence = jax.random.permutation(stream_key, number_of)
    crowded, ordinary = load_shares(number_of, rows * top, limit, skew, True), load_shares(number_of, rows * top, limit, skew, False)
    places = jnp.arange(number_of)

    def named(sizes, turn):
        used = int((sizes > 0).sum())
        fixed = max(1, used // 4)
        passed = fixed + (places - fixed + turn * (used - fixed)) % max(1, number_of - fixed)
        return jnp.zeros((number_of,), jnp.int32).at[sequence[jnp.where(places < fixed, places, passed)]].set(jnp.asarray(sizes, jnp.int32))

    sizes = jnp.where(number % 4 == 0, named(crowded, number // 4), named(ordinary, number - number // 4 - 1))
    mixed = jax.random.permutation(jax.random.fold_in(own, 3), number_of)
    giver, receiver = mixed[0:number_of // 2 * 2:2], mixed[1:number_of // 2 * 2:2]
    margin = jnp.minimum(sizes[giver] - 1, limit - sizes[receiver]) // 2
    margin = jnp.where((giver == sequence[0]) | (receiver == sequence[0]) | (sizes[receiver] == 0), 0, jnp.maximum(margin, 0))
    passed = jax.random.randint(jax.random.fold_in(own, 4), (number_of // 2,), 0, 1 << 20) % (margin + 1)
    sizes = sizes.at[giver].add(-passed).at[receiver].add(passed)
    members = jnp.searchsorted(jnp.cumsum(sizes), jnp.arange(rows * top), side="right").astype(jnp.int32)
    listing = members.reshape(top, rows).T
    listing = listing[jax.random.permutation(jax.random.fold_in(own, 1), rows)]
    turn = jax.random.randint(jax.random.fold_in(own, 2), (rows, 1), 0, top)
    return jnp.take_along_axis(listing, (jnp.arange(top)[None, :] + turn) % top, axis=1)


def load_shares(number_of, total, reach, lean, full):
    loads = [(1 << 20) // math.isqrt(rank ** lean) + 1 for rank in range(1, number_of + 1)]
    largest = reach if full else min(reach, max(-(-total // number_of), total * loads[0] // sum(loads)))
    least = 1 if total - largest >= number_of - 1 else 0
    given, spare = [largest] + [least] * (number_of - 1), total - largest - least * (number_of - 1)
    while spare > 0:
        free = [i for i in range(1, number_of) if given[i] < largest] or [i for i in range(1, number_of) if given[i] < reach]
        pool, remaining = sum([loads[i] for i in free]), spare
        for i in free:
            more = min(reach - given[i], max(1, remaining * loads[i] // pool), spare)
            given[i] = given[i] + more
            spare = spare - more
    return np.array(given)


def noise(own_key, dims, spread, bound, split=(), kind=jnp.bfloat16):
    level = level_of(own_key, dims, split, -0.22, 0.18) if split else 1.0
    entries = jax.random.normal(own_key, dims, jnp.float32) * spread * level
    return jnp.minimum(jnp.maximum(entries, -bound), bound).astype(kind)


def setup_inputs(seed: int = 0) -> dict:
    splits = jax.random.split(jax.random.key(seed), 9)
    positions = jnp.clip(jax.random.uniform(splits[0], (3, RAYS, SAMPLES), jnp.float32, -1.0, 1.0) * level_of(splits[0], (3, RAYS, SAMPLES), ((1, 256),), -0.4, 0.0), -1.0, 1.0)
    spacing = jnp.clip(jnp.exp(math.log(0.15) - 2.3025852 * jax.random.uniform(splits[1], (RAYS, SAMPLES), jnp.float32) ** level_of(splits[1], (RAYS, SAMPLES), ((0, 256),), -0.2, 0.2)), 0.015, 0.15)
    targets = jnp.clip(1.0 * jax.random.uniform(splits[2], (3, RAYS), jnp.float32) ** level_of(splits[2], (3, RAYS), ((1, 256),), -0.2, 0.2), 0.0, 1.0)
    frequencies = noise(splits[3], (3, ENC // 2), 2.0, 12.0, (), jnp.float32)
    seg_region_keys = jax.random.split(jax.random.fold_in(splits[4], 1), SEGMENTS // SEG_DEV)
    seg_region_turns = jax.random.permutation(jax.random.fold_in(splits[4], 3), SEGMENTS // SEG_DEV)
    seg_region = jax.vmap(lambda own, number: deal_out(jax.random.fold_in(splits[4], 2), own, number, SEG_DEV, REGIONS, 1, CAP, 2))(seg_region_keys, seg_region_turns).reshape((SEGMENTS, 1))
    w_in = noise(splits[5], (REGIONS, ENC, HID), ENC ** -0.5, 0.5, ((0, 16),))
    w_hidden = noise(splits[6], (REGIONS, LAYERS, HID, HID), HID ** -0.5, 0.375, ((0, 16),))
    w_head = noise(splits[7], (REGIONS, 4, HID), (HID // 9) ** -0.5, 1.0, ((0, 16),))
    return dict(positions=positions, spacing=spacing, targets=targets, frequencies=frequencies, seg_region=seg_region, w_in=w_in, w_hidden=w_hidden, w_head=w_head)


LOSS_GAIN = 64.0
BLOCK_SEGS = 256

def encode(points, frequencies):
    angle = 2.0 * jnp.pi * jnp.dot(points.T, frequencies, precision=lax.Precision.HIGHEST)
    return jnp.concatenate([jnp.sin(angle), jnp.cos(angle)], axis=1).astype(jnp.bfloat16)

def silu_slope(preact):
    sigm = jax.nn.sigmoid(preact)
    return sigm * (1.0 + preact * (1.0 - sigm))

def forward(features, first_weight, hidden_weight, head_weight):
    preacts = []
    activations = [features]
    preact = jnp.dot(features, first_weight, preferred_element_type=jnp.float32)
    preacts.append(preact)
    current = jax.nn.silu(preact).astype(jnp.bfloat16)
    activations.append(current)
    for layer_index in range(hidden_weight.shape[0]):
        preact = jnp.dot(current, hidden_weight[layer_index], preferred_element_type=jnp.float32)
        preacts.append(preact)
        current = jax.nn.silu(preact).astype(jnp.bfloat16)
        activations.append(current)
    raw_out = lax.dot_general(head_weight, current, (((1,), (1,)), ((), ())), preferred_element_type=jnp.float32)
    return (raw_out, preacts, activations)

def backward(upstream, preacts, activations, hidden_weight, head_weight):
    gradient = upstream.astype(jnp.bfloat16)
    head_grad = lax.dot_general(gradient, activations[-1], (((1,), (0,)), ((), ())), preferred_element_type=jnp.float32)
    flowing = lax.dot_general(gradient, head_weight, (((0,), (0,)), ((), ())), preferred_element_type=jnp.float32)
    hidden_grads = []
    for layer_index in reversed(range(hidden_weight.shape[0])):
        gradient = (flowing * silu_slope(preacts[layer_index + 1])).astype(jnp.bfloat16)
        hidden_grads.insert(0, lax.dot_general(activations[layer_index + 1], gradient, (((0,), (0,)), ((), ())), preferred_element_type=jnp.float32))
        flowing = lax.dot_general(gradient, hidden_weight[layer_index], (((1,), (1,)), ((), ())), preferred_element_type=jnp.float32)
    gradient = (flowing * silu_slope(preacts[0])).astype(jnp.bfloat16)
    first_grad = lax.dot_general(activations[0], gradient, (((0,), (0,)), ((), ())), preferred_element_type=jnp.float32)
    return (first_grad, jnp.stack(hidden_grads), head_grad)

def render(density, tint_rgb, spacing):
    depths = density * spacing
    running = jnp.cumsum(depths, axis=-1)
    transmit = jnp.exp(depths - running)
    weight = transmit * -jnp.expm1(-depths)
    return lax.optimization_barrier(jnp.sum(tint_rgb * weight[None], axis=-1))

def reference(positions, spacing, targets, frequencies, seg_region, w_in, w_hidden, w_head):
    region_ids = seg_region[:, 0].astype(jnp.int32)
    member = (region_ids[:, None] == jnp.arange(REGIONS, dtype=jnp.int32)[None, :]).astype(jnp.int32)
    counts = lax.optimization_barrier(jnp.sum(member, axis=0)).astype(jnp.int32)
    padded = (counts + BLOCK_SEGS - 1) // BLOCK_SEGS * BLOCK_SEGS
    block_ends = jnp.cumsum(padded).astype(jnp.int32)
    starts = block_ends - padded
    firsts = (jnp.cumsum(counts) - counts).astype(jnp.int32)
    sort_order = jnp.argsort(region_ids, stable=True).astype(jnp.int32)
    sorted_ids = region_ids[sort_order]
    placement = starts[sorted_ids] + jnp.arange(SEGMENTS, dtype=jnp.int32) - firsts[sorted_ids]
    blocks = (SEGMENTS + BLOCK_SEGS - 1) // BLOCK_SEGS + REGIONS
    block_table = jnp.full((blocks * BLOCK_SEGS,), -1, jnp.int32).at[placement].set(sort_order)
    block_table = block_table.reshape(blocks, BLOCK_SEGS)
    block_starts = jnp.arange(blocks, dtype=jnp.int32) * BLOCK_SEGS
    block_region = jnp.minimum(lax.optimization_barrier(jnp.sum((block_ends[None, :] <= block_starts[:, None]).astype(jnp.int32), axis=1)), REGIONS - 1).astype(jnp.int32)
    seg_points = positions.reshape(3, SEGMENTS, SEG_LEN)

    def run(block_index):
        block_row = block_table[block_index]
        region = block_region[block_index]
        chosen = jnp.maximum(block_row, 0)
        sample_points = seg_points[:, chosen].reshape(3, BLOCK_SEGS * SEG_LEN)
        features = encode(sample_points, frequencies)
        return forward(features, w_in[region], w_hidden[region], w_head[region])
    raw_blocks = lax.map(lambda block_index: run(block_index)[0], jnp.arange(blocks, dtype=jnp.int32))
    raw_seg = raw_blocks.reshape(blocks, 4, BLOCK_SEGS, SEG_LEN).transpose(1, 0, 2, 3).reshape(4, blocks * BLOCK_SEGS, SEG_LEN)
    target_index = jnp.where(block_table >= 0, block_table, SEGMENTS).reshape(-1)
    raw_all = jnp.zeros((4, SEGMENTS + 1, SEG_LEN), jnp.float32).at[:, target_index].set(raw_seg)[:, :SEGMENTS]
    raw_rays = raw_all.reshape(4, RAYS, SAMPLES)

    def shade(raw_in):
        return render(jax.nn.softplus(raw_in[0]), jax.nn.sigmoid(raw_in[1:]), spacing)
    pixel_color, pullback = jax.vjp(shade, raw_rays)
    loss_gain = LOSS_GAIN / math.sqrt(RAYS)
    raw_grad, = pullback((pixel_color - targets) * loss_gain)
    grad_seg = raw_grad.reshape(4, SEGMENTS, SEG_LEN)
    valid = (block_table >= 0).reshape(-1).astype(jnp.float32)
    grad_blocks = grad_seg[:, jnp.maximum(block_table, 0).reshape(-1)] * valid[None, :, None]
    grad_blocks = grad_blocks.reshape(4, blocks, BLOCK_SEGS * SEG_LEN).transpose(1, 0, 2)

    def step(carry, block_index):
        region = block_region[block_index]
        raw_out, preacts, activations = run(block_index)
        first_grad, hidden_grad, head_grad = backward(grad_blocks[block_index], preacts, activations, w_hidden[region], w_head[region])
        return ((carry[0].at[region].add(first_grad), carry[1].at[region].add(hidden_grad), carry[2].at[region].add(head_grad)), None)
    initial = (jnp.zeros((REGIONS, ENC, HID), jnp.float32), jnp.zeros((REGIONS, LAYERS, HID, HID), jnp.float32), jnp.zeros((REGIONS, 4, HID), jnp.float32))
    totals, unused = lax.scan(step, initial, jnp.arange(blocks, dtype=jnp.int32))
    return (pixel_color, totals[0], totals[1], totals[2])
```

```python
import math

import jax
import jax.numpy as jnp
from jax import lax
from jax.experimental import pallas as pl
from jax.experimental.pallas import tpu as pltpu
from jax.sharding import PartitionSpec as P

LOSS_GAIN = 64.0
F32 = jnp.float32
BF16 = jnp.bfloat16
NN = (((1,), (0,)), ((), ()))
NT = (((1,), (1,)), ((), ()))
TN = (((0,), (0,)), ((), ()))
VMEM_LIMIT = 48 * 1024 * 1024

REGIONS = 16
SEGS = 64
SEG_LEN = 32
CAP = 8
SLOTS = REGIONS * CAP
RAYS_DEV = 16
ROWS = SLOTS * SEG_LEN
ENC = 128
HID = 256
LAYERS = 4
BLOCK = 80


def iota(shape, axis):
    return lax.broadcasted_iota(jnp.int32, shape, axis)


def dot(a, b, dims=NN):
    return lax.dot_general(a, b, dims, preferred_element_type=F32)


def split3(x):
    hi = x.astype(BF16)
    rest = x - hi.astype(F32)
    mid = rest.astype(BF16)
    low = (rest - mid.astype(F32)).astype(BF16)
    return hi, mid, low


def pick(x, onehot, dims):
    hi, mid, low = split3(x)
    return dot(hi, onehot, dims) + (dot(mid, onehot, dims) + dot(low, onehot, dims))


def pick_left(onehot, x, dims):
    hi, mid, low = split3(x)
    return dot(onehot, hi, dims) + (dot(onehot, mid, dims) + dot(onehot, low, dims))


def as_mask(cond):
    return jnp.where(cond, 1.0, 0.0).astype(BF16)


def dispatch_kernel(me_ref, pos_ref, sp_ref, tg_ref, seg_ref, send_ref, meta_ref):
    parity = me_ref[0] % 2
    seg = seg_ref[...]
    lane = iota((SEGS, SLOTS), 1)
    member = jnp.where(seg == lane, 1.0, 0.0)
    earlier = as_mask(iota((SEGS, SEGS), 1) < iota((SEGS, SEGS), 0))
    rank = dot(earlier, member.astype(BF16))
    slot = jnp.sum(member * (rank + (lane * CAP).astype(F32)), axis=1, keepdims=True)
    onehot = as_mask(slot == lane.astype(F32))
    row = iota((SEGS, SEGS), 0)
    order = as_mask(iota((SEGS, SEGS), 1) == (row % RAYS_DEV) * 4 + row // RAYS_DEV)
    onehot = dot(order, onehot).astype(BF16)
    parts = []
    for q in range(4):
        cut = slice(q * SEG_LEN, (q + 1) * SEG_LEN)
        parts.append(
            jnp.concatenate(
                [pos_ref[0, :, cut], pos_ref[1, :, cut], pos_ref[2, :, cut], sp_ref[:, cut]], axis=1
            )
        )
    data = jnp.concatenate(parts, axis=0)
    send_ref[...] = pick_left(onehot, data, TN)
    ids = dot(iota((8, SLOTS), 1).astype(BF16), onehot, NT)
    half = iota((8, 128), 1) // SEGS == parity
    ids = jnp.concatenate([ids, ids], axis=1)
    meta_ref[0:1, :] = jnp.where(half, ids, 0.0)[0:1]
    spread = as_mask(iota((RAYS_DEV, 128), 1) % RAYS_DEV == iota((RAYS_DEV, 128), 0))
    tg = pick(jnp.concatenate([tg_ref[...], tg_ref[...], tg_ref[0:2, :]], axis=0), spread, NN)
    meta_ref[1:4, :] = jnp.where(half, tg, 0.0)[0:3]


def dispatch(me, positions, spacing, targets, seg_region):
    return pl.pallas_call(
        dispatch_kernel,
        in_specs=[pl.BlockSpec(memory_space=pltpu.SMEM)] + [pl.BlockSpec(memory_space=pltpu.VMEM)] * 4,
        out_shape=(
            jax.ShapeDtypeStruct((SLOTS, 128), F32),
            jax.ShapeDtypeStruct((4, 128), F32),
        ),
        name="dispatch",
    )(me, positions, spacing, targets, seg_region)


def encode(pos, freq, first, count):
    cols = []
    for t in range(count):
        at = first + t
        cols.append(
            (freq[:, 0:1] * pos(0, at) + freq[:, 1:2] * pos(1, at)) + freq[:, 2:3] * pos(2, at)
        )
    turns = jnp.concatenate(cols, axis=1)
    quarter = jnp.floor(turns + 0.5)
    x = turns - quarter
    y = x * x
    sine = x * (1.5707963268 + y * (-0.6459640975 + y * (0.0796926262 + y * (-0.0046817541 + y * 0.0001604412))))
    cosine = 1.0 + y * (-1.2337005501 + y * (0.2536695079 + y * (-0.0208634807 + y * (0.0009192602 - y * 0.0000252020))))
    whole = quarter.astype(jnp.int32)
    odd = (whole & 1) == 1
    first_part = jnp.where(odd, cosine, sine)
    second_part = jnp.where(odd, sine, cosine)
    first_part = jnp.where((whole & 2) == 2, -first_part, first_part)
    second_part = jnp.where(((whole + 1) & 2) == 2, -second_part, second_part)
    return jnp.concatenate([first_part, second_part], axis=0).astype(BF16)


def local_render(raw, spacing):
    value = raw[0]
    small = jnp.exp(-jnp.abs(value))
    log1p = jnp.where(
        small < 0.02,
        small * (1.0 - small * (0.5 - small * (1.0 / 3.0 - small * 0.25))),
        jnp.log(1.0 + small),
    )
    density = jnp.maximum(value, 0.0) + log1p
    depth = density * spacing
    before = as_mask(iota((SEG_LEN, SEG_LEN), 1) < iota((SEG_LEN, SEG_LEN), 0))
    transmit = jnp.exp(-pick_left(before, depth, NN))
    fade = jnp.exp(-depth)
    opaque = jnp.where(
        depth < 0.03,
        depth * (1.0 - depth * (0.5 - depth * (1.0 / 6.0 - depth * (1.0 / 24.0)))),
        1.0 - fade,
    )
    weight = transmit * opaque
    tints = [0.5 + 0.5 * jnp.tanh(0.5 * raw[c]) for c in (1, 2, 3)]
    return depth, transmit, fade, weight, tints


def layer(weight, act):
    half = dot(weight, act)
    return half, jnp.tanh(half)


def forward_kernel(
    recv_ref, meta_ref, freq_ref, win_ref, wh_ref, head_ref, raw_ref, send_ref, pos_ref, *, chunk
):
    step = pl.program_id(0)
    count = chunk // SLOTS

    @pl.when(step == 0)
    def _():
        pos_ref[...] = jnp.transpose(recv_ref[...])

    def pos(c, at):
        return pos_ref[pl.ds(c * SEG_LEN + at, 1), :]

    current = encode(pos, freq_ref[...], step * count, count)
    for index in range(LAYERS + 1):
        half, tanh = layer(win_ref[...] if index == 0 else wh_ref[index - 1], current)
        current = (half + half * tanh).astype(BF16)
    raw = dot(head_ref[...], current)
    for t in range(count):
        for c in range(4):
            raw_ref[c, pl.ds(step * count + t, 1), :] = raw[c : c + 1, t * SLOTS : (t + 1) * SLOTS]

    @pl.when(step == pl.num_programs(0) - 1)
    def _():
        depth, transmit, fade, weight, tints = local_render(
            [raw_ref[c] for c in range(4)], pos_ref[3 * SEG_LEN : 4 * SEG_LEN, :]
        )
        rows = [jnp.sum(depth, axis=0, keepdims=True)]
        rows += [jnp.sum(weight * tint, axis=0, keepdims=True) for tint in tints]
        block = jnp.concatenate(rows + [meta_ref[...]], axis=0)
        for r in range(REGIONS):
            send_ref[r] = block


def whole(shape):
    zeros = (0,) * len(shape)
    return pl.BlockSpec(shape, lambda i: zeros)


def forward_call(recv, meta, freq, win_t, wh_t, head, chunk=1024):
    kernel = lambda *refs: forward_kernel(*refs, chunk=chunk)
    return pl.pallas_call(
        kernel,
        grid=(ROWS // chunk,),
        in_specs=[whole(x.shape) for x in (recv, meta, freq, win_t, wh_t, head)],
        out_specs=(whole((4, SEG_LEN, SLOTS)), whole((REGIONS, 8, SLOTS))),
        out_shape=(
            jax.ShapeDtypeStruct((4, SEG_LEN, SLOTS), F32),
            jax.ShapeDtypeStruct((REGIONS, 8, SLOTS), F32),
        ),
        scratch_shapes=[pltpu.VMEM((128, SLOTS), F32)],
        compiler_params=pltpu.CompilerParams(vmem_limit_bytes=VMEM_LIMIT),
        cost_estimate=pl.CostEstimate(flops=2 * ROWS * 296000, bytes_accessed=700000, transcendentals=ROWS * 1280),
        name="forward",
    )(recv, meta, freq, win_t, wh_t, head)


def keep_kernel(recv_ref, freq_ref, win_ref, wh_ref, enc_ref, act_ref, slope_ref, pos_ref, *, chunk):
    step = pl.program_id(0)
    count = chunk // SLOTS

    @pl.when(step == 0)
    def _():
        pos_ref[...] = jnp.transpose(recv_ref[...])

    def pos(c, at):
        return pos_ref[pl.ds(c * SEG_LEN + at, 1), :]

    current = encode(pos, freq_ref[...], step * count, count)
    enc_ref[...] = current
    for index in range(LAYERS + 1):
        half, tanh = layer(win_ref[...] if index == 0 else wh_ref[index - 1], current)
        part = half * tanh
        current = (half + part).astype(BF16)
        act_ref[index] = current
        slope_ref[index] = ((1.0 + tanh) + (half - part * tanh)).astype(BF16)


def keep_call(recv, freq, win_t, wh_t, chunk=512):
    kernel = lambda *refs: keep_kernel(*refs, chunk=chunk)
    count = LAYERS + 1
    return pl.pallas_call(
        kernel,
        grid=(ROWS // chunk,),
        in_specs=[whole(x.shape) for x in (recv, freq, win_t, wh_t)],
        out_specs=(
            pl.BlockSpec((ENC, chunk), lambda i: (0, i)),
            pl.BlockSpec((count, HID, chunk), lambda i: (0, 0, i)),
            pl.BlockSpec((count, HID, chunk), lambda i: (0, 0, i)),
        ),
        out_shape=(
            jax.ShapeDtypeStruct((ENC, ROWS), BF16),
            jax.ShapeDtypeStruct((count, HID, ROWS), BF16),
            jax.ShapeDtypeStruct((count, HID, ROWS), BF16),
        ),
        scratch_shapes=[pltpu.VMEM((128, SLOTS), F32)],
        compiler_params=pltpu.CompilerParams(vmem_limit_bytes=VMEM_LIMIT),
        cost_estimate=pl.CostEstimate(flops=2 * ROWS * 296000, bytes_accessed=22000000, transcendentals=ROWS * 1280),
        name="keep",
    )(recv, freq, win_t, wh_t)


def composite(me, got, gain):
    pairs = REGIONS // 2
    values = jnp.concatenate([got[r] for r in range(REGIONS)], axis=0)
    hi, mid, low = split3(values)
    lane = iota((1, 128), 1)
    sub = iota((128, 128), 0)
    depth_rows, colour_rows, target_rows, onehots = [], [[], [], []], [[], [], []], []
    for m in range(pairs):
        meta = got[2 * m, 4:8, :] + got[2 * m + 1, 4:8, :]
        ids = meta[0:1, :].astype(jnp.int32)
        owner = ids // CAP
        place = (2 * m + lane // SEGS) * CAP + ids % CAP
        onehot = sub == place
        picked = as_mask(onehot)
        found = dot(hi, picked) + (dot(mid, picked) + dot(low, picked))
        total = jnp.zeros((8, 128), F32)
        for r in range(REGIONS):
            total = total + jnp.where(owner == r, found[8 * r : 8 * r + 8], 0.0)
        depth_rows.append(total[0:1])
        for c in range(3):
            colour_rows[c].append(total[1 + c : 2 + c])
            target_rows[c].append(meta[1 + c : 2 + c])
        onehots.append(as_mask(jnp.logical_and(onehot, owner == me)))
    depth = jnp.concatenate(depth_rows, axis=0)
    colours = [jnp.concatenate(rows, axis=0) for rows in colour_rows]
    targets = [jnp.concatenate(rows, axis=0) for rows in target_rows]
    within = iota((pairs, 128), 1) % SEGS

    def earlier(x):
        total = jnp.zeros_like(x)
        for k in (1, 2, 3):
            total = total + jnp.where(within >= k * RAYS_DEV, pltpu.roll(x, k * RAYS_DEV, 1), 0.0)
        return total

    def later(x):
        total = jnp.zeros_like(x)
        for k in (1, 2, 3):
            total = total + jnp.where(within < SEGS - k * RAYS_DEV, pltpu.roll(x, 128 - k * RAYS_DEV, 1), 0.0)
        return total

    transmit = jnp.exp(-earlier(depth))
    behind = jnp.zeros((pairs, 128), F32)
    pixels, scaled = [], []
    for c in range(3):
        weighted = transmit * colours[c]
        after = later(weighted)
        pixel = (earlier(weighted) + weighted) + after
        pull = (pixel - targets[c]) * gain
        behind = behind + pull * after
        scaled.append(transmit * pull)
        pixels.append(pixel)
    rows = scaled + [behind]
    slots = jnp.zeros((32, SLOTS), F32)
    for m in range(pairs):
        x = jnp.concatenate([r[m : m + 1] for r in rows] + [jnp.zeros((4, 128), F32)], axis=0)
        parts = jnp.concatenate([p.astype(F32) for p in split3(x)] + [jnp.zeros((8, 128), F32)], axis=0)
        slots = slots + dot(parts.astype(BF16), onehots[m], NT)
    slots = slots[0:8] + (slots[8:16] + slots[16:24])
    own = []
    mine = jnp.logical_and(iota((pairs, 128), 0) == me // 2, iota((pairs, 128), 1) // SEGS == me % 2)
    for c in range(3):
        row = jnp.sum(jnp.where(mine, pixels[c], 0.0), axis=0, keepdims=True)
        own.append((row + pltpu.roll(row, SEGS, 1))[:, 0:RAYS_DEV])
    return slots, jnp.concatenate(own, axis=0)


def backward_kernel(
    me_ref, got_ref, recv_ref, raw_ref, enc_ref, act_ref, slope_ref, wh_ref, head_ref,
    pix_ref, keep_ref, send_ref, up_ref, gin_ref, gh_ref, ghead_ref, *, chunk, gain,
):
    step = pl.program_id(0)

    @pl.when(step == 0)
    def _():
        got = got_ref[...]
        slots, pixel = composite(me_ref[0], got, gain)
        pix_ref[...] = pixel
        spacing = jnp.transpose(recv_ref[...])[3 * SEG_LEN : 4 * SEG_LEN, :]
        raw = [raw_ref[c] for c in range(4)]
        depth, transmit, fade, weight, tints = local_render(raw, spacing)
        pull = jnp.zeros((SEG_LEN, SLOTS), F32)
        for c in range(3):
            pull = pull + slots[c : c + 1] * tints[c]
        after = as_mask(iota((SEG_LEN, SEG_LEN), 1) > iota((SEG_LEN, SEG_LEN), 0))
        rest = pick_left(after, weight * pull, NN) + slots[3:4]
        slope = 0.5 + 0.5 * jnp.tanh(0.5 * raw[0])
        ups = [(transmit * fade * pull - rest) * spacing * slope]
        ups += [slots[c : c + 1] * weight * (tints[c] * (1.0 - tints[c])) for c in range(3)]
        up_ref[...] = jnp.zeros_like(up_ref)
        for c in range(4):
            for t in range(SEG_LEN):
                up_ref[c : c + 1, t * SLOTS : (t + 1) * SLOTS] = ups[c][t : t + 1]
        gin_ref[...] = jnp.zeros_like(gin_ref)
        gh_ref[...] = jnp.zeros_like(gh_ref)
        ghead_ref[...] = jnp.zeros_like(ghead_ref)

    up = up_ref[:, pl.ds(pl.multiple_of(step * chunk, chunk), chunk)].astype(BF16)
    ghead_ref[...] += dot(up, act_ref[LAYERS], NT)
    flow = dot(head_ref[...], up)
    for index in range(LAYERS, 0, -1):
        back = (flow * slope_ref[index].astype(F32)).astype(BF16)
        gh_ref[index - 1] += dot(act_ref[index - 1], back, NT)
        flow = dot(wh_ref[index - 1], back)
    back = (flow * slope_ref[0].astype(F32)).astype(BF16)
    gin_ref[...] += dot(enc_ref[...], back, NT)

    @pl.when(step == pl.num_programs(0) - 1)
    def _():
        core = me_ref[1]
        for ref, which in ((keep_ref, core), (send_ref, 1 - core)):
            for z in range(8):
                to = z * 2 + which
                for l in range(LAYERS):
                    rows = gh_ref[l, pl.ds(pl.multiple_of(to * 16, 16), 16), :]
                    ref[z, l * 16 : (l + 1) * 16, :] = rows.astype(BF16)
                rows = gin_ref[pl.ds(pl.multiple_of(to * 8, 8), 8), :]
                ref[z, 64:80, :] = jnp.concatenate([rows, ghead_ref[...]], axis=0).astype(BF16)


def backward_call(me, got, recv, raw, enc, act, slope, wh, head, gain, chunk=512):
    kernel = lambda *refs: backward_kernel(*refs, chunk=chunk, gain=gain)
    count = LAYERS + 1
    return pl.pallas_call(
        kernel,
        grid=(ROWS // chunk,),
        in_specs=[
            pl.BlockSpec(memory_space=pltpu.SMEM),
            whole(got.shape),
            whole(recv.shape),
            whole(raw.shape),
            pl.BlockSpec((ENC, chunk), lambda i: (0, i)),
            pl.BlockSpec((count, HID, chunk), lambda i: (0, 0, i)),
            pl.BlockSpec((count, HID, chunk), lambda i: (0, 0, i)),
            whole(wh.shape),
            whole(head.shape),
        ],
        out_specs=(whole((3, RAYS_DEV)), whole((8, BLOCK, HID)), whole((8, BLOCK, HID))),
        out_shape=(
            jax.ShapeDtypeStruct((3, RAYS_DEV), F32),
            jax.ShapeDtypeStruct((8, BLOCK, HID), BF16),
            jax.ShapeDtypeStruct((8, BLOCK, HID), BF16),
        ),
        scratch_shapes=[
            pltpu.VMEM((8, ROWS), F32),
            pltpu.VMEM((ENC, HID), F32),
            pltpu.VMEM((LAYERS, HID, HID), F32),
            pltpu.VMEM((8, HID), F32),
        ],
        compiler_params=pltpu.CompilerParams(vmem_limit_bytes=VMEM_LIMIT),
        cost_estimate=pl.CostEstimate(flops=4 * ROWS * 296000, bytes_accessed=23000000, transcendentals=0),
        name="backward",
    )(me, got, recv, raw, enc, act, slope, wh, head)


def total_kernel(got_ref, head_at_ref, gin_ref, gh_ref, ghead_ref):
    total = got_ref[0].astype(F32)
    for z in range(1, 8):
        total = total + got_ref[z].astype(F32)
    for l in range(LAYERS):
        gh_ref[0, l] = total[l * 16 : (l + 1) * 16]
    gin_ref[0] = total[64:72]
    mine = iota((HID, 16), 0) == head_at_ref[0] * 16 + iota((HID, 16), 1)
    ghead_ref[0] = pick(total[72:80], as_mask(mine), NN)[0:4]


def total_call(got, dp_at):
    return pl.pallas_call(
        total_kernel,
        in_specs=[pl.BlockSpec(memory_space=pltpu.VMEM), pl.BlockSpec(memory_space=pltpu.SMEM)],
        out_shape=(
            jax.ShapeDtypeStruct((1, 8, HID), F32),
            jax.ShapeDtypeStruct((1, LAYERS, 16, HID), F32),
            jax.ShapeDtypeStruct((1, 4, 16), F32),
        ),
        name="total",
    )(got, dp_at)


def per_device(positions, spacing, targets, frequencies, seg_region, w_in, w_hidden, w_head):
    region = lax.axis_index("region")
    dp = lax.axis_index("dp")
    where = jnp.stack([region, dp % 2]).astype(jnp.int32)
    rays = spacing.shape[0] * lax.axis_size("region") * lax.axis_size("dp")
    gain = LOSS_GAIN / math.sqrt(rays)

    half = jnp.asarray(0.5, BF16)
    win_t = w_in[0].T * half
    wh_t = jnp.transpose(w_hidden[0], (0, 2, 1)) * half
    wh_half = w_hidden[0] * half
    head = w_head[0]
    head_t = jnp.pad(head, ((0, 4), (0, 0))).T * half
    freq = 4.0 * frequencies.T

    outgoing, meta = dispatch(where, positions, spacing, targets, seg_region)
    arrived = lax.all_to_all(
        outgoing.reshape(REGIONS, CAP, 128), "region", split_axis=0, concat_axis=0, tiled=True
    ).reshape(SLOTS, 128)
    raw, summary = forward_call(arrived, meta, freq, win_t, wh_t, head)
    got = lax.all_to_all(summary, "region", split_axis=0, concat_axis=0, tiled=True)
    enc, act, slope = keep_call(arrived, freq, win_t, wh_t)
    pixel_color, keep, send = backward_call(
        where, got, arrived, raw, enc, act, slope, wh_half, head_t, gain
    )
    other = lax.ppermute(send, "dp", [(i, i ^ 1) for i in range(16)])
    both = (keep.astype(F32) + other.astype(F32)).astype(BF16)
    groups = [list(range(0, 16, 2)), list(range(1, 16, 2))]
    parts = lax.all_to_all(both, "dp", 0, 0, tiled=True, axis_index_groups=groups)
    grad_in, grad_hidden, grad_head = total_call(parts, dp.reshape(1).astype(jnp.int32))
    return pixel_color, grad_in, grad_hidden, grad_head


def solution(mesh):
    return jax.shard_map(
        per_device,
        mesh=mesh,
        in_specs=(
            P(None, ("region", "dp"), None),
            P(("region", "dp"), None),
            P(None, ("region", "dp")),
            P(),
            P(("region", "dp"), None),
            P("region", None, None),
            P("region", None, None, None),
            P("region", None, None),
        ),
        out_specs=(
            P(None, ("region", "dp")),
            P("region", "dp", None),
            P("region", None, "dp", None),
            P("region", None, "dp"),
        ),
        check_vma=False,
    )
```

```python
import math

import jax
import jax.numpy as jnp
from jax import lax
from jax.experimental import pallas as pl
from jax.experimental.pallas import tpu as pltpu
from jax.sharding import PartitionSpec as P

LOSS_GAIN = 64.0
F32 = jnp.float32
BF16 = jnp.bfloat16
NN = (((1,), (0,)), ((), ()))
NT = (((1,), (1,)), ((), ()))
TN = (((0,), (0,)), ((), ()))
VMEM_LIMIT = 40 * 1024 * 1024

REGIONS = 16
SEGS = 64
SEG_LEN = 32
CAP = 8
SLOTS = REGIONS * CAP
RAYS_DEV = 16
ROWS = SLOTS * SEG_LEN
ENC = 128
HID = 256
LAYERS = 4
BLOCK = 80

SIN = (3.141592588, -5.167707194, 2.550035118, -0.5980627511, 0.07724868669)
COS = (0.9999999532, -4.934792829, 4.058411309, -1.331876237, 0.219688854)


def iota(shape, axis):
    return lax.broadcasted_iota(jnp.int32, shape, axis)


def dot(a, b, dims=NN):
    return lax.dot_general(a, b, dims, preferred_element_type=F32)


def split3(x):
    hi = x.astype(BF16)
    rest = x - hi.astype(F32)
    mid = rest.astype(BF16)
    low = (rest - mid.astype(F32)).astype(BF16)
    return hi, mid, low


def pick(x, onehot, dims):
    hi, mid, low = split3(x)
    return dot(hi, onehot, dims) + (dot(mid, onehot, dims) + dot(low, onehot, dims))


def pick_left(onehot, x, dims):
    hi, mid, low = split3(x)
    return dot(onehot, hi, dims) + (dot(onehot, mid, dims) + dot(onehot, low, dims))


def as_mask(cond):
    return jnp.where(cond, 1.0, 0.0).astype(BF16)


def dispatch_kernel(pos_ref, sp_ref, tg_ref, seg_ref, send_ref, meta_ref):
    parity = lax.axis_index("region") % 2
    lane = iota((SEGS, SLOTS), 1)
    row = iota((SEGS, SEGS), 0)
    order = as_mask(iota((SEGS, SEGS), 1) == (row % RAYS_DEV) * 4 + row // RAYS_DEV)
    seg = dot(order, jnp.broadcast_to(seg_ref[...], (8, SEGS)).astype(F32).astype(BF16), NT)[:, 0:1]
    member = jnp.where(seg == lane.astype(F32), 1.0, 0.0)
    earlier = as_mask(iota((SEGS, SEGS), 1) < row)
    rank = dot(earlier, member.astype(BF16))
    slot = jnp.sum(member * (rank + (lane * CAP).astype(F32)), axis=1, keepdims=True)
    onehot = as_mask(slot == lane.astype(F32))
    parts = []
    for q in range(4):
        cut = slice(q * SEG_LEN, (q + 1) * SEG_LEN)
        parts.append(
            jnp.concatenate(
                [pos_ref[0, :, cut], pos_ref[1, :, cut], pos_ref[2, :, cut], sp_ref[:, cut]], axis=1
            )
        )
    data = jnp.concatenate(parts, axis=0)
    send_ref[...] = pick_left(onehot, data, TN)
    ids = dot(iota((8, SLOTS), 1).astype(BF16), onehot, NT)
    half = iota((8, 128), 1) // SEGS == parity
    ids = jnp.concatenate([ids, ids], axis=1)
    spread = as_mask(iota((RAYS_DEV, 128), 1) % RAYS_DEV == iota((RAYS_DEV, 128), 0))
    tg = pick(jnp.concatenate([tg_ref[...], tg_ref[...], tg_ref[0:2, :]], axis=0), spread, NN)
    meta_ref[...] = jnp.where(half, jnp.concatenate([ids[0:4], ids[0:1], tg[0:3]], axis=0), 0.0)


def dispatch(positions, spacing, targets, seg_region):
    return pl.pallas_call(
        dispatch_kernel,
        in_specs=[pl.BlockSpec(memory_space=pltpu.VMEM)] * 4,
        out_shape=(
            jax.ShapeDtypeStruct((SLOTS, 128), F32),
            pltpu.HBM((8, 128), F32),
        ),
        name="dispatch",
    )(positions, spacing, targets, seg_region)


def encode(pos, freq, first, count):
    cols = []
    for t in range(count):
        at = first + t
        cols.append(
            (freq[:, 0:1] * pos(0, at) + freq[:, 1:2] * pos(1, at)) + freq[:, 2:3] * pos(2, at)
        )
    turns = jnp.concatenate(cols, axis=1)
    x = turns - jnp.floor(turns + 0.5)
    y = x * x
    sine = x * (SIN[0] + y * (SIN[1] + y * (SIN[2] + y * (SIN[3] + y * SIN[4]))))
    cosine = COS[0] + y * (COS[1] + y * (COS[2] + y * (COS[3] + y * COS[4])))
    twice = sine + sine
    return jnp.concatenate([twice * cosine, 1.0 - twice * sine], axis=0).astype(BF16)


def local_render(raw, spacing):
    value = raw[0]
    small = jnp.exp(-jnp.abs(value))
    log1p = jnp.where(
        small < 0.02,
        small * (1.0 - small * (0.5 - small * (1.0 / 3.0 - small * 0.25))),
        jnp.log(1.0 + small),
    )
    density = jnp.maximum(value, 0.0) + log1p
    depth = density * spacing
    before = as_mask(iota((SEG_LEN, SEG_LEN), 1) < iota((SEG_LEN, SEG_LEN), 0))
    transmit = jnp.exp(-pick_left(before, depth, NN))
    fade = jnp.exp(-depth)
    opaque = jnp.where(
        depth < 0.03,
        depth * (1.0 - depth * (0.5 - depth * (1.0 / 6.0 - depth * (1.0 / 24.0)))),
        1.0 - fade,
    )
    weight = transmit * opaque
    tints = [0.5 + 0.5 * jnp.tanh(0.5 * raw[c]) for c in (1, 2, 3)]
    return depth, transmit, fade, weight, tints


def forward_kernel(
    recv_ref, meta_ref, freq_ref, win_ref, wh_ref, head_ref,
    send_ref, enc_ref, half_ref, local_ref,
    pos_ref, raw_ref, meta_copy, halves, encoded, local, sem, out_sem, *, chunk,
):
    meta = pltpu.make_async_copy(meta_ref, meta_copy, sem)
    meta.start()
    pos_ref[...] = jnp.transpose(recv_ref[...])
    count = chunk // SLOTS

    def pos(c, at):
        return pos_ref[c * SEG_LEN + at : c * SEG_LEN + at + 1, :]

    starts = range(0, ROWS, chunk)
    acts = []
    for start in starts:
        acts.append(encode(pos, freq_ref[...], start // SLOTS, count))
        encoded[:, start : start + chunk] = acts[-1]
    copies = [pltpu.make_async_copy(encoded, enc_ref, out_sem.at[LAYERS + 1])]
    copies[-1].start()
    for index in range(LAYERS + 1):
        weight = win_ref[...] if index == 0 else wh_ref[index - 1]
        for i, start in enumerate(starts):
            half = dot(weight, acts[i])
            acts[i] = (half + half * jnp.tanh(half)).astype(BF16)
            halves[index, :, start : start + chunk] = half.astype(BF16)
        copies.append(pltpu.make_async_copy(halves.at[index], half_ref.at[index], out_sem.at[index]))
        copies[-1].start()
    for i, act in enumerate(acts):
        raw = dot(head_ref[...], act)
        for t in range(count):
            for c in range(4):
                raw_ref[c, i * count + t : i * count + t + 1, :] = raw[c : c + 1, t * SLOTS : (t + 1) * SLOTS]
    raw = [raw_ref[c] for c in range(4)]
    spacing = pos_ref[3 * SEG_LEN : 4 * SEG_LEN, :]
    depth, transmit, fade, weight, tints = local_render(raw, spacing)
    rows = [jnp.sum(depth, axis=0, keepdims=True)]
    rows += [jnp.sum(weight * tint, axis=0, keepdims=True) for tint in tints]
    meta.wait()
    block = jnp.concatenate(rows + [meta_copy[4:8, :]], axis=0)
    for r in range(REGIONS):
        send_ref[r] = block
    steep = (0.5 + 0.5 * jnp.tanh(0.5 * raw[0])) * spacing
    local[0] = transmit * fade * steep
    local[1] = steep
    for c in range(3):
        local[2 + c] = tints[c]
        local[5 + c] = weight * (tints[c] * (1.0 - tints[c]))
    local[8] = weight
    copies.append(pltpu.make_async_copy(local, local_ref, out_sem.at[LAYERS + 2]))
    copies[-1].start()
    for copy in copies:
        copy.wait()


def in_vmem(count):
    return [pl.BlockSpec(memory_space=pltpu.VMEM)] * count


def in_hbm(count):
    return [pl.BlockSpec(memory_space=pltpu.HBM)] * count


def forward_call(recv, meta, freq, win_t, wh_t, head, chunk=2048):
    kernel = lambda *refs: forward_kernel(*refs, chunk=chunk)
    specs = in_vmem(6)
    specs[1] = in_hbm(1)[0]
    meta = pltpu.with_memory_space_constraint(meta, pltpu.HBM)
    return pl.pallas_call(
        kernel,
        in_specs=specs,
        out_shape=(
            jax.ShapeDtypeStruct((REGIONS, 8, SLOTS), F32),
            pltpu.HBM((ENC, ROWS), BF16),
            pltpu.HBM((LAYERS + 1, HID, ROWS), BF16),
            pltpu.HBM((9, SEG_LEN, SLOTS), F32),
        ),
        out_specs=tuple(in_vmem(1) + in_hbm(3)),
        scratch_shapes=[
            pltpu.VMEM((128, SLOTS), F32),
            pltpu.VMEM((4, SEG_LEN, SLOTS), F32),
            pltpu.VMEM((8, SLOTS), F32),
            pltpu.VMEM((LAYERS + 1, HID, ROWS), BF16),
            pltpu.VMEM((ENC, ROWS), BF16),
            pltpu.VMEM((9, SEG_LEN, SLOTS), F32),
            pltpu.SemaphoreType.DMA,
            pltpu.SemaphoreType.DMA((LAYERS + 3,)),
        ],
        compiler_params=pltpu.CompilerParams(vmem_limit_bytes=VMEM_LIMIT),
        cost_estimate=pl.CostEstimate(flops=2 * ROWS * 296000, bytes_accessed=700000, transcendentals=ROWS * 1280),
        name="forward",
    )(recv, meta, freq, win_t, wh_t, head)


def composite(me, got, gain):
    pairs = REGIONS // 2
    values = jnp.concatenate([got[r] for r in range(REGIONS)], axis=0)
    hi, mid, low = split3(values)
    lane = iota((1, 128), 1)
    sub = iota((128, 128), 0)
    depth_rows, colour_rows, target_rows, onehots = [], [[], [], []], [[], [], []], []
    for m in range(pairs):
        meta = got[2 * m, 4:8, :] + got[2 * m + 1, 4:8, :]
        ids = meta[0:1, :].astype(jnp.int32)
        owner = ids // CAP
        place = (2 * m + lane // SEGS) * CAP + ids % CAP
        onehot = sub == place
        picked = as_mask(onehot)
        found = dot(hi, picked) + (dot(mid, picked) + dot(low, picked))
        total = jnp.zeros((8, 128), F32)
        for r in range(REGIONS):
            total = total + jnp.where(owner == r, found[8 * r : 8 * r + 8], 0.0)
        depth_rows.append(total[0:1])
        for c in range(3):
            colour_rows[c].append(total[1 + c : 2 + c])
            target_rows[c].append(meta[1 + c : 2 + c])
        onehots.append(as_mask(jnp.logical_and(onehot, owner == me)))
    depth = jnp.concatenate(depth_rows, axis=0)
    colours = [jnp.concatenate(rows, axis=0) for rows in colour_rows]
    targets = [jnp.concatenate(rows, axis=0) for rows in target_rows]
    within = iota((pairs, 128), 1) % SEGS

    def earlier(x):
        total = jnp.zeros_like(x)
        for k in (1, 2, 3):
            total = total + jnp.where(within >= k * RAYS_DEV, pltpu.roll(x, k * RAYS_DEV, 1), 0.0)
        return total

    def later(x):
        total = jnp.zeros_like(x)
        for k in (1, 2, 3):
            total = total + jnp.where(within < SEGS - k * RAYS_DEV, pltpu.roll(x, 128 - k * RAYS_DEV, 1), 0.0)
        return total

    transmit = jnp.exp(-earlier(depth))
    behind = jnp.zeros((pairs, 128), F32)
    pixels, scaled = [], []
    for c in range(3):
        weighted = transmit * colours[c]
        after = later(weighted)
        pixel = (earlier(weighted) + weighted) + after
        pull = (pixel - targets[c]) * gain
        behind = behind + pull * after
        scaled.append(transmit * pull)
        pixels.append(pixel)
    rows = scaled + [behind]
    slots = jnp.zeros((32, SLOTS), F32)
    for m in range(pairs):
        x = jnp.concatenate([r[m : m + 1] for r in rows] + [jnp.zeros((4, 128), F32)], axis=0)
        parts = jnp.concatenate([p.astype(F32) for p in split3(x)] + [jnp.zeros((8, 128), F32)], axis=0)
        slots = slots + dot(parts.astype(BF16), onehots[m], NT)
    slots = slots[0:8] + (slots[8:16] + slots[16:24])
    own = []
    mine = jnp.logical_and(iota((pairs, 128), 0) == me // 2, iota((pairs, 128), 1) // SEGS == me % 2)
    for c in range(3):
        row = jnp.sum(jnp.where(mine, pixels[c], 0.0), axis=0, keepdims=True)
        own.append((row + pltpu.roll(row, SEGS, 1))[:, 0:RAYS_DEV])
    return slots, jnp.concatenate(own, axis=0)


def backward_kernel(
    got_ref, wh_ref, head_ref, local_in, enc_in, half_in,
    pix_ref, keep_ref, send_ref, up_ref, gin_ref, gh_ref, halves, enc_ref, local_ref, in_sem, *, chunk, gain,
):
    copies = [
        pltpu.make_async_copy(half_in.at[index], halves.at[index], in_sem.at[index])
        for index in range(LAYERS + 1)
    ]
    local_copy = pltpu.make_async_copy(local_in, local_ref, in_sem.at[LAYERS + 1])
    enc_copy = pltpu.make_async_copy(enc_in, enc_ref, in_sem.at[LAYERS + 2])
    for copy in [local_copy] + copies[::-1] + [enc_copy]:
        copy.start()
    slots, pixel = composite(lax.axis_index("region"), got_ref, gain)
    pix_ref[...] = pixel
    local_copy.wait()
    pull = jnp.zeros((SEG_LEN, SLOTS), F32)
    for c in range(3):
        pull = pull + slots[c : c + 1] * local_ref[2 + c]
    after = as_mask(iota((SEG_LEN, SEG_LEN), 1) > iota((SEG_LEN, SEG_LEN), 0))
    rest = pick_left(after, local_ref[8] * pull, NN) + slots[3:4]
    ups = [local_ref[0] * pull - rest * local_ref[1]]
    ups += [slots[c : c + 1] * local_ref[5 + c] for c in range(3)]
    up_ref[...] = jnp.zeros_like(up_ref)
    for c in range(4):
        for t in range(SEG_LEN):
            up_ref[c : c + 1, t * SLOTS : (t + 1) * SLOTS] = ups[c][t : t + 1]

    cuts = [slice(start, start + chunk) for start in range(0, ROWS, chunk)]

    def residual(index, cut):
        half = halves[index, :, cut]
        tanh = jnp.tanh(half)
        above = 1.0 + tanh
        return half * above, above + half * (above * (1.0 - tanh))

    copies[LAYERS].wait()
    flows, slopes = [], []
    ghead = jnp.zeros((8, HID), F32)
    for cut in cuts:
        up = up_ref[:, cut].astype(BF16)
        flows.append(dot(head_ref[...], up))
        act, slope = residual(LAYERS, cut)
        slopes.append(slope)
        ghead = ghead + dot(up, act, NT)
    for index in range(LAYERS, -1, -1):
        if index > 0:
            copies[index - 1].wait()
        else:
            enc_copy.wait()
        total = None
        for i, cut in enumerate(cuts):
            back = flows[i].astype(BF16) * slopes[i]
            if index > 0:
                flows[i] = dot(wh_ref[index - 1], back)
                act, slopes[i] = residual(index - 1, cut)
            else:
                act = enc_ref[:, cut]
            part = dot(act, back, NT)
            total = part if total is None else total + part
        if index > 0:
            gh_ref[index - 1] = total
        else:
            gin_ref[...] = total
    core = lax.axis_index("dp") % 2
    for ref, which in ((keep_ref, core), (send_ref, 1 - core)):
        for z in range(8):
            to = z * 2 + which
            for l in range(LAYERS):
                rows = gh_ref[l, pl.ds(pl.multiple_of(to * 16, 16), 16), :]
                ref[z, l * 16 : (l + 1) * 16, :] = rows.astype(BF16)
            rows = gin_ref[pl.ds(pl.multiple_of(to * 8, 8), 8), :]
            ref[z, 64:80, :] = jnp.concatenate([rows, ghead], axis=0).astype(BF16)


def backward_call(got, wh, head, local, enc, half, gain, chunk=2048):
    held = [pltpu.with_memory_space_constraint(x, pltpu.HBM) for x in (local, enc, half)]
    kernel = lambda *refs: backward_kernel(*refs, chunk=chunk, gain=gain)
    return pl.pallas_call(
        kernel,
        in_specs=in_vmem(3) + in_hbm(3),
        out_shape=(
            jax.ShapeDtypeStruct((3, RAYS_DEV), F32),
            jax.ShapeDtypeStruct((8, BLOCK, HID), BF16),
            jax.ShapeDtypeStruct((8, BLOCK, HID), BF16),
        ),
        scratch_shapes=[
            pltpu.VMEM((8, ROWS), F32),
            pltpu.VMEM((ENC, HID), F32),
            pltpu.VMEM((LAYERS, HID, HID), F32),
            pltpu.VMEM((LAYERS + 1, HID, ROWS), BF16),
            pltpu.VMEM((ENC, ROWS), BF16),
            pltpu.VMEM((9, SEG_LEN, SLOTS), F32),
            pltpu.SemaphoreType.DMA((LAYERS + 3,)),
        ],
        compiler_params=pltpu.CompilerParams(vmem_limit_bytes=VMEM_LIMIT),
        cost_estimate=pl.CostEstimate(flops=4 * ROWS * 296000, bytes_accessed=23000000, transcendentals=0),
        name="backward",
    )(got, wh, head, *held)


def total_kernel(got_ref, gin_ref, gh_ref, ghead_ref):
    total = got_ref[0].astype(F32)
    for z in range(1, 8):
        total = total + got_ref[z].astype(F32)
    for l in range(LAYERS):
        gh_ref[0, l] = total[l * 16 : (l + 1) * 16]
    gin_ref[0] = total[64:72]
    mine = iota((HID, 16), 0) == lax.axis_index("dp") * 16 + iota((HID, 16), 1)
    ghead_ref[0] = pick(total[72:80], as_mask(mine), NN)[0:4]


def total_call(got):
    return pl.pallas_call(
        total_kernel,
        in_specs=in_vmem(1),
        out_shape=(
            jax.ShapeDtypeStruct((1, 8, HID), F32),
            jax.ShapeDtypeStruct((1, LAYERS, 16, HID), F32),
            jax.ShapeDtypeStruct((1, 4, 16), F32),
        ),
        name="total",
    )(got)


def per_device(positions, spacing, targets, frequencies, seg_region, w_in, w_hidden, w_head):
    rays = spacing.shape[0] * lax.axis_size("region") * lax.axis_size("dp")
    gain = LOSS_GAIN / math.sqrt(rays)

    half = jnp.asarray(0.5, BF16)
    win_t = w_in[0].T * half
    wh_t = jnp.transpose(w_hidden[0], (0, 2, 1)) * half
    wh_half = w_hidden[0] * half
    head = w_head[0]
    head_t = jnp.pad(head, ((0, 4), (0, 0))).T * half
    freq = frequencies.T

    outgoing, meta = dispatch(positions, spacing, targets, seg_region.reshape(1, SEGS))
    arrived = lax.all_to_all(
        outgoing.reshape(REGIONS, CAP, 128), "region", split_axis=0, concat_axis=0, tiled=True
    ).reshape(SLOTS, 128)
    summary, enc, half_pre, local = forward_call(arrived, meta, freq, win_t, wh_t, head)
    got = lax.all_to_all(summary, "region", split_axis=0, concat_axis=0, tiled=True)
    pixel_color, keep, send = backward_call(got, wh_half, head_t, local, enc, half_pre, gain)
    other = lax.ppermute(send, "dp", [(i, i ^ 1) for i in range(16)])
    both = (keep.astype(F32) + other.astype(F32)).astype(BF16)
    groups = [list(range(0, 16, 2)), list(range(1, 16, 2))]
    parts = lax.all_to_all(both, "dp", 0, 0, tiled=True, axis_index_groups=groups)
    grad_in, grad_hidden, grad_head = total_call(parts)
    return pixel_color, grad_in, grad_hidden, grad_head


def solution(mesh):
    return jax.shard_map(
        per_device,
        mesh=mesh,
        in_specs=(
            P(None, ("region", "dp"), None),
            P(("region", "dp"), None),
            P(None, ("region", "dp")),
            P(),
            P(("region", "dp"), None),
            P("region", None, None),
            P("region", None, None, None),
            P("region", None, None),
        ),
        out_specs=(
            P(None, ("region", "dp")),
            P("region", "dp", None),
            P("region", None, "dp", None),
            P("region", None, "dp"),
        ),
        check_vma=False,
    )
```

```python
import math

import jax
import jax.numpy as jnp
from jax import lax
from jax.experimental import pallas as pl
from jax.experimental.pallas import tpu as pltpu
from jax.sharding import PartitionSpec as P

LOSS_GAIN = 64.0
F32 = jnp.float32
BF16 = jnp.bfloat16
NN = (((1,), (0,)), ((), ()))
NT = (((1,), (1,)), ((), ()))
TN = (((0,), (0,)), ((), ()))
VMEM_LIMIT = 40 * 1024 * 1024
BACK_LIMIT = 24 * 1024 * 1024

REGIONS = 16
SEGS = 64
SEG_LEN = 32
CAP = 8
SLOTS = REGIONS * CAP
RAYS_DEV = 16
ROWS = SLOTS * SEG_LEN
ENC = 128
HID = 256
LAYERS = 4
BLOCK = 80

SIN = (3.141592588, -5.167707194, 2.550035118, -0.5980627511, 0.07724868669)
COS = (0.9999999532, -4.934792829, 4.058411309, -1.331876237, 0.219688854)


def iota(shape, axis):
    return lax.broadcasted_iota(jnp.int32, shape, axis)


def dot(a, b, dims=NN):
    return lax.dot_general(a, b, dims, preferred_element_type=F32)


def split3(x):
    hi = x.astype(BF16)
    rest = x - hi.astype(F32)
    mid = rest.astype(BF16)
    low = (rest - mid.astype(F32)).astype(BF16)
    return hi, mid, low


def pick(x, onehot, dims):
    hi, mid, low = split3(x)
    return dot(hi, onehot, dims) + (dot(mid, onehot, dims) + dot(low, onehot, dims))


def pick_left(onehot, x, dims):
    hi, mid, low = split3(x)
    return dot(onehot, hi, dims) + (dot(onehot, mid, dims) + dot(onehot, low, dims))


def as_mask(cond):
    return jnp.where(cond, 1.0, 0.0).astype(BF16)


def dispatch_kernel(pos_ref, sp_ref, tg_ref, seg_ref, send_ref, meta_ref):
    parity = lax.axis_index("region") % 2
    lane = iota((SEGS, SLOTS), 1)
    row = iota((SEGS, SEGS), 0)
    order = as_mask(iota((SEGS, SEGS), 1) == (row % RAYS_DEV) * 4 + row // RAYS_DEV)
    seg = dot(order, jnp.broadcast_to(seg_ref[...], (8, SEGS)).astype(F32).astype(BF16), NT)[:, 0:1]
    member = jnp.where(seg == lane.astype(F32), 1.0, 0.0)
    earlier = as_mask(iota((SEGS, SEGS), 1) < row)
    rank = dot(earlier, member.astype(BF16))
    slot = jnp.sum(member * (rank + (lane * CAP).astype(F32)), axis=1, keepdims=True)
    onehot = as_mask(slot == lane.astype(F32))
    parts = []
    for q in range(4):
        cut = slice(q * SEG_LEN, (q + 1) * SEG_LEN)
        parts.append(
            jnp.concatenate(
                [pos_ref[0, :, cut], pos_ref[1, :, cut], pos_ref[2, :, cut], sp_ref[:, cut]], axis=1
            )
        )
    data = jnp.concatenate(parts, axis=0)
    send_ref[...] = pick_left(onehot, data, TN)
    ids = dot(iota((8, SLOTS), 1).astype(BF16), onehot, NT)
    half = iota((8, 128), 1) // SEGS == parity
    ids = jnp.concatenate([ids, ids], axis=1)
    spread = as_mask(iota((RAYS_DEV, 128), 1) % RAYS_DEV == iota((RAYS_DEV, 128), 0))
    tg = pick(jnp.concatenate([tg_ref[...], tg_ref[...], tg_ref[0:2, :]], axis=0), spread, NN)
    meta_ref[...] = jnp.where(half, jnp.concatenate([ids[0:4], ids[0:1], tg[0:3]], axis=0), 0.0)


def dispatch(positions, spacing, targets, seg_region):
    return pl.pallas_call(
        dispatch_kernel,
        in_specs=[pl.BlockSpec(memory_space=pltpu.VMEM)] * 4,
        out_shape=(
            jax.ShapeDtypeStruct((SLOTS, 128), F32),
            pltpu.HBM((8, 128), F32),
        ),
        name="dispatch",
    )(positions, spacing, targets, seg_region)


def encode(pos, freq, first, count):
    cols = []
    for t in range(count):
        at = first + t
        cols.append(
            (freq[:, 0:1] * pos(0, at) + freq[:, 1:2] * pos(1, at)) + freq[:, 2:3] * pos(2, at)
        )
    turns = jnp.concatenate(cols, axis=1)
    x = turns - jnp.floor(turns + 0.5)
    y = x * x
    sine = x * (SIN[0] + y * (SIN[1] + y * (SIN[2] + y * (SIN[3] + y * SIN[4]))))
    cosine = COS[0] + y * (COS[1] + y * (COS[2] + y * (COS[3] + y * COS[4])))
    twice = sine + sine
    return jnp.concatenate([twice * cosine, 1.0 - twice * sine], axis=0).astype(BF16)


def local_render(raw, spacing):
    value = raw[0]
    small = jnp.exp(-jnp.abs(value))
    log1p = jnp.where(
        small < 0.02,
        small * (1.0 - small * (0.5 - small * (1.0 / 3.0 - small * 0.25))),
        jnp.log(1.0 + small),
    )
    density = jnp.maximum(value, 0.0) + log1p
    depth = density * spacing
    before = as_mask(iota((SEG_LEN, SEG_LEN), 1) < iota((SEG_LEN, SEG_LEN), 0))
    transmit = jnp.exp(-pick_left(before, depth, NN))
    fade = jnp.exp(-depth)
    opaque = jnp.where(
        depth < 0.03,
        depth * (1.0 - depth * (0.5 - depth * (1.0 / 6.0 - depth * (1.0 / 24.0)))),
        1.0 - fade,
    )
    weight = transmit * opaque
    tints = [0.5 + 0.5 * jnp.tanh(0.5 * raw[c]) for c in (1, 2, 3)]
    return depth, transmit, fade, weight, tints


def forward_kernel(
    recv_ref, meta_ref, freq_ref, win_ref, wh_ref, head_ref,
    send_ref, enc_ref, half_ref, local_ref,
    pos_ref, raw_ref, meta_copy, halves, encoded, local, sem, out_sem, *, chunk,
):
    meta = pltpu.make_async_copy(meta_ref, meta_copy, sem)
    meta.start()
    pos_ref[...] = jnp.transpose(recv_ref[...])
    count = chunk // SLOTS

    def pos(c, at):
        return pos_ref[c * SEG_LEN + at : c * SEG_LEN + at + 1, :]

    starts = range(0, ROWS, chunk)
    acts = []
    for start in starts:
        acts.append(encode(pos, freq_ref[...], start // SLOTS, count))
        encoded[:, start : start + chunk] = acts[-1]
    copies = [pltpu.make_async_copy(encoded, enc_ref, out_sem.at[LAYERS + 1])]
    copies[-1].start()
    for index in range(LAYERS + 1):
        weight = win_ref[...] if index == 0 else wh_ref[index - 1]
        for i, start in enumerate(starts):
            half = dot(weight, acts[i])
            acts[i] = (half + half * jnp.tanh(half)).astype(BF16)
            halves[index, :, start : start + chunk] = half.astype(BF16)
        copies.append(pltpu.make_async_copy(halves.at[index], half_ref.at[index], out_sem.at[index]))
        copies[-1].start()
    for i, act in enumerate(acts):
        raw = dot(head_ref[...], act)
        for t in range(count):
            for c in range(4):
                raw_ref[c, i * count + t : i * count + t + 1, :] = raw[c : c + 1, t * SLOTS : (t + 1) * SLOTS]
    raw = [raw_ref[c] for c in range(4)]
    spacing = pos_ref[3 * SEG_LEN : 4 * SEG_LEN, :]
    depth, transmit, fade, weight, tints = local_render(raw, spacing)
    rows = [jnp.sum(depth, axis=0, keepdims=True)]
    rows += [jnp.sum(weight * tint, axis=0, keepdims=True) for tint in tints]
    meta.wait()
    block = jnp.concatenate(rows + [meta_copy[4:8, :]], axis=0)
    for r in range(REGIONS):
        send_ref[r] = block
    steep = (0.5 + 0.5 * jnp.tanh(0.5 * raw[0])) * spacing
    local[0] = transmit * fade * steep
    local[1] = steep
    for c in range(3):
        local[2 + c] = tints[c]
        local[5 + c] = weight * (tints[c] * (1.0 - tints[c]))
    local[8] = weight
    copies.append(pltpu.make_async_copy(local, local_ref, out_sem.at[LAYERS + 2]))
    copies[-1].start()
    for copy in copies:
        copy.wait()


def in_vmem(count):
    return [pl.BlockSpec(memory_space=pltpu.VMEM)] * count


def in_hbm(count):
    return [pl.BlockSpec(memory_space=pltpu.HBM)] * count


def forward_call(recv, meta, freq, win_t, wh_t, head, chunk=2048):
    kernel = lambda *refs: forward_kernel(*refs, chunk=chunk)
    specs = in_vmem(6)
    specs[1] = in_hbm(1)[0]
    meta = pltpu.with_memory_space_constraint(meta, pltpu.HBM)
    return pl.pallas_call(
        kernel,
        in_specs=specs,
        out_shape=(
            jax.ShapeDtypeStruct((REGIONS, 8, SLOTS), F32),
            pltpu.HBM((ENC, ROWS), BF16),
            pltpu.HBM((LAYERS + 1, HID, ROWS), BF16),
            pltpu.HBM((9, SEG_LEN, SLOTS), F32),
        ),
        out_specs=tuple(in_vmem(1) + in_hbm(3)),
        scratch_shapes=[
            pltpu.VMEM((128, SLOTS), F32),
            pltpu.VMEM((4, SEG_LEN, SLOTS), F32),
            pltpu.VMEM((8, SLOTS), F32),
            pltpu.VMEM((LAYERS + 1, HID, ROWS), BF16),
            pltpu.VMEM((ENC, ROWS), BF16),
            pltpu.VMEM((9, SEG_LEN, SLOTS), F32),
            pltpu.SemaphoreType.DMA,
            pltpu.SemaphoreType.DMA((LAYERS + 3,)),
        ],
        compiler_params=pltpu.CompilerParams(vmem_limit_bytes=VMEM_LIMIT),
        cost_estimate=pl.CostEstimate(flops=2 * ROWS * 296000, bytes_accessed=700000, transcendentals=ROWS * 1280),
        name="forward",
    )(recv, meta, freq, win_t, wh_t, head)


def composite(me, got, gain):
    pairs = REGIONS // 2
    values = jnp.concatenate([got[r] for r in range(REGIONS)], axis=0)
    hi, mid, low = split3(values)
    lane = iota((1, 128), 1)
    sub = iota((128, 128), 0)
    depth_rows, colour_rows, target_rows, onehots = [], [[], [], []], [[], [], []], []
    for m in range(pairs):
        meta = got[2 * m, 4:8, :] + got[2 * m + 1, 4:8, :]
        ids = meta[0:1, :].astype(jnp.int32)
        owner = ids // CAP
        place = (2 * m + lane // SEGS) * CAP + ids % CAP
        onehot = sub == place
        picked = as_mask(onehot)
        found = dot(hi, picked) + (dot(mid, picked) + dot(low, picked))
        total = jnp.zeros((8, 128), F32)
        for r in range(REGIONS):
            total = total + jnp.where(owner == r, found[8 * r : 8 * r + 8], 0.0)
        depth_rows.append(total[0:1])
        for c in range(3):
            colour_rows[c].append(total[1 + c : 2 + c])
            target_rows[c].append(meta[1 + c : 2 + c])
        onehots.append(as_mask(jnp.logical_and(onehot, owner == me)))
    depth = jnp.concatenate(depth_rows, axis=0)
    colours = [jnp.concatenate(rows, axis=0) for rows in colour_rows]
    targets = [jnp.concatenate(rows, axis=0) for rows in target_rows]
    within = iota((pairs, 128), 1) % SEGS

    def earlier(x):
        total = jnp.zeros_like(x)
        for k in (1, 2, 3):
            total = total + jnp.where(within >= k * RAYS_DEV, pltpu.roll(x, k * RAYS_DEV, 1), 0.0)
        return total

    def later(x):
        total = jnp.zeros_like(x)
        for k in (1, 2, 3):
            total = total + jnp.where(within < SEGS - k * RAYS_DEV, pltpu.roll(x, 128 - k * RAYS_DEV, 1), 0.0)
        return total

    transmit = jnp.exp(-earlier(depth))
    behind = jnp.zeros((pairs, 128), F32)
    pixels, scaled = [], []
    for c in range(3):
        weighted = transmit * colours[c]
        after = later(weighted)
        pixel = (earlier(weighted) + weighted) + after
        pull = (pixel - targets[c]) * gain
        behind = behind + pull * after
        scaled.append(transmit * pull)
        pixels.append(pixel)
    rows = scaled + [behind]
    slots = jnp.zeros((32, SLOTS), F32)
    for m in range(pairs):
        x = jnp.concatenate([r[m : m + 1] for r in rows] + [jnp.zeros((4, 128), F32)], axis=0)
        parts = jnp.concatenate([p.astype(F32) for p in split3(x)] + [jnp.zeros((8, 128), F32)], axis=0)
        slots = slots + dot(parts.astype(BF16), onehots[m], NT)
    slots = slots[0:8] + (slots[8:16] + slots[16:24])
    own = []
    mine = jnp.logical_and(iota((pairs, 128), 0) == me // 2, iota((pairs, 128), 1) // SEGS == me % 2)
    for c in range(3):
        row = jnp.sum(jnp.where(mine, pixels[c], 0.0), axis=0, keepdims=True)
        own.append((row + pltpu.roll(row, SEGS, 1))[:, 0:RAYS_DEV])
    return slots, jnp.concatenate(own, axis=0)


def residual_of(half):
    tanh = jnp.tanh(half)
    above = 1.0 + tanh
    return half * above, above + half * (above * (1.0 - tanh))


def fetch_kernel(local_in, half_in, local_ref, top_ref, sem):
    copies = [
        pltpu.make_async_copy(half_in.at[LAYERS], top_ref, sem.at[0]),
        pltpu.make_async_copy(local_in, local_ref, sem.at[1]),
    ]
    for copy in copies:
        copy.start()
    for copy in copies:
        copy.wait()


def fetch_call(local, half):
    return pl.pallas_call(
        fetch_kernel,
        in_specs=in_hbm(2),
        out_specs=tuple(in_vmem(2)),
        out_shape=(
            jax.ShapeDtypeStruct((9, SEG_LEN, SLOTS), F32),
            jax.ShapeDtypeStruct((HID, ROWS), BF16),
        ),
        scratch_shapes=[pltpu.SemaphoreType.DMA((2,))],
        compiler_params=pltpu.CompilerParams(vmem_limit_bytes=16 * 1024 * 1024),
        cost_estimate=pl.CostEstimate(flops=2 * 10**9, bytes_accessed=2 * 10**7, transcendentals=0),
        name="fetch",
    )(*[pltpu.with_memory_space_constraint(x, pltpu.HBM) for x in (local, half)])


def backward_kernel(
    got_ref, wh_ref, head_ref, local_ref, top_ref, enc_in, half_in,
    pix_ref, keep_ref, send_ref, up_ref, gin_ref, gh_ref, halves, enc_ref, in_sem, *, chunk, gain,
):
    copies = [
        pltpu.make_async_copy(half_in.at[index], halves.at[index], in_sem.at[index]) for index in range(LAYERS)
    ]
    copies.append(pltpu.make_async_copy(enc_in, enc_ref, in_sem.at[LAYERS]))
    for copy in copies[LAYERS - 1 :: -1] + copies[LAYERS:]:
        copy.start()
    slots, pixel = composite(lax.axis_index("region"), got_ref, gain)
    pix_ref[...] = pixel
    pull = jnp.zeros((SEG_LEN, SLOTS), F32)
    for c in range(3):
        pull = pull + slots[c : c + 1] * local_ref[2 + c]
    after = as_mask(iota((SEG_LEN, SEG_LEN), 1) > iota((SEG_LEN, SEG_LEN), 0))
    rest = pick_left(after, local_ref[8] * pull, NN) + slots[3:4]
    ups = [local_ref[0] * pull - rest * local_ref[1]]
    ups += [slots[c : c + 1] * local_ref[5 + c] for c in range(3)]
    up_ref[...] = jnp.zeros_like(up_ref)
    for c in range(4):
        for t in range(SEG_LEN):
            up_ref[c : c + 1, t * SLOTS : (t + 1) * SLOTS] = ups[c][t : t + 1]

    cuts = [slice(start, start + chunk) for start in range(0, ROWS, chunk)]

    def residual(index, cut):
        half = top_ref[:, cut] if index == LAYERS else halves[index, :, cut]
        return residual_of(half)

    flows, slopes = [], []
    ghead = jnp.zeros((8, HID), F32)
    for cut in cuts:
        up = up_ref[:, cut].astype(BF16)
        flows.append(dot(head_ref[...], up))
        act, slope = residual(LAYERS, cut)
        slopes.append(slope)
        ghead = ghead + dot(up, act, NT)
    for index in range(LAYERS, -1, -1):
        for copy in {LAYERS: copies[LAYERS - 1 : LAYERS], LAYERS - 1: copies[1 : LAYERS - 1], 1: [copies[0], copies[LAYERS]]}.get(index, []):
            copy.wait()
        total = None
        for i, cut in enumerate(cuts):
            back = flows[i].astype(BF16) * slopes[i]
            if index > 0:
                flows[i] = dot(wh_ref[index - 1], back)
                act, slopes[i] = residual(index - 1, cut)
            else:
                act = enc_ref[:, cut]
            part = dot(act, back, NT)
            total = part if total is None else total + part
        if index > 0:
            gh_ref[index - 1] = total
        else:
            gin_ref[...] = total
    core = lax.axis_index("dp") % 2
    for ref, which in ((keep_ref, core), (send_ref, 1 - core)):
        for z in range(8):
            to = z * 2 + which
            for l in range(LAYERS):
                rows = gh_ref[l, pl.ds(pl.multiple_of(to * 16, 16), 16), :]
                ref[z, l * 16 : (l + 1) * 16, :] = rows.astype(BF16)
            rows = gin_ref[pl.ds(pl.multiple_of(to * 8, 8), 8), :]
            ref[z, 64:80, :] = jnp.concatenate([rows, ghead], axis=0).astype(BF16)


def backward_call(got, wh, head, local, top, enc, half, gain, chunk=512):
    enc, half = [pltpu.with_memory_space_constraint(x, pltpu.HBM) for x in (enc, half)]
    kernel = lambda *refs: backward_kernel(*refs, chunk=chunk, gain=gain)
    return pl.pallas_call(
        kernel,
        in_specs=in_vmem(5) + in_hbm(2),
        out_shape=(
            jax.ShapeDtypeStruct((3, RAYS_DEV), F32),
            jax.ShapeDtypeStruct((8, BLOCK, HID), BF16),
            jax.ShapeDtypeStruct((8, BLOCK, HID), BF16),
        ),
        scratch_shapes=[
            pltpu.VMEM((8, ROWS), F32),
            pltpu.VMEM((ENC, HID), F32),
            pltpu.VMEM((LAYERS, HID, HID), F32),
            pltpu.VMEM((LAYERS, HID, ROWS), BF16),
            pltpu.VMEM((ENC, ROWS), BF16),
            pltpu.SemaphoreType.DMA((LAYERS + 1,)),
        ],
        compiler_params=pltpu.CompilerParams(vmem_limit_bytes=BACK_LIMIT),
        cost_estimate=pl.CostEstimate(flops=4 * ROWS * 296000, bytes_accessed=23000000, transcendentals=0),
        name="backward",
    )(got, wh, head, local, top, enc, half)


def total_kernel(got_ref, gin_ref, gh_ref, ghead_ref):
    total = got_ref[0].astype(F32)
    for z in range(1, 8):
        total = total + got_ref[z].astype(F32)
    for l in range(LAYERS):
        gh_ref[0, l] = total[l * 16 : (l + 1) * 16]
    gin_ref[0] = total[64:72]
    mine = iota((HID, 16), 0) == lax.axis_index("dp") * 16 + iota((HID, 16), 1)
    ghead_ref[0] = pick(total[72:80], as_mask(mine), NN)[0:4]


def total_call(got):
    return pl.pallas_call(
        total_kernel,
        in_specs=in_vmem(1),
        out_shape=(
            jax.ShapeDtypeStruct((1, 8, HID), F32),
            jax.ShapeDtypeStruct((1, LAYERS, 16, HID), F32),
            jax.ShapeDtypeStruct((1, 4, 16), F32),
        ),
        name="total",
    )(got)


def per_device(positions, spacing, targets, frequencies, seg_region, w_in, w_hidden, w_head):
    rays = spacing.shape[0] * lax.axis_size("region") * lax.axis_size("dp")
    gain = LOSS_GAIN / math.sqrt(rays)

    half = jnp.asarray(0.5, BF16)
    win_t = w_in[0].T * half
    wh_t = jnp.transpose(w_hidden[0], (0, 2, 1)) * half
    wh_half = w_hidden[0] * half
    head = w_head[0]
    head_t = jnp.pad(head, ((0, 4), (0, 0))).T * half
    freq = frequencies.T

    outgoing, meta = dispatch(positions, spacing, targets, seg_region.reshape(1, SEGS))
    arrived = lax.all_to_all(
        outgoing.reshape(REGIONS, CAP, 128), "region", split_axis=0, concat_axis=0, tiled=True
    ).reshape(SLOTS, 128)
    summary, enc, half_pre, local = forward_call(arrived, meta, freq, win_t, wh_t, head)
    got = lax.all_to_all(summary, "region", split_axis=0, concat_axis=0, tiled=True)
    local, top = fetch_call(local, half_pre)
    pixel_color, keep, send = backward_call(got, wh_half, head_t, local, top, enc, half_pre, gain)
    other = lax.ppermute(send, "dp", [(i, i ^ 1) for i in range(16)])
    both = (keep.astype(F32) + other.astype(F32)).astype(BF16)
    groups = [list(range(0, 16, 2)), list(range(1, 16, 2))]
    parts = lax.all_to_all(both, "dp", 0, 0, tiled=True, axis_index_groups=groups)
    grad_in, grad_hidden, grad_head = total_call(parts)
    return pixel_color, grad_in, grad_hidden, grad_head


def solution(mesh):
    return jax.shard_map(
        per_device,
        mesh=mesh,
        in_specs=(
            P(None, ("region", "dp"), None),
            P(("region", "dp"), None),
            P(None, ("region", "dp")),
            P(),
            P(("region", "dp"), None),
            P("region", None, None),
            P("region", None, None, None),
            P("region", None, None),
        ),
        out_specs=(
            P(None, ("region", "dp")),
            P("region", "dp", None),
            P("region", None, "dp", None),
            P("region", None, "dp"),
        ),
        check_vma=False,
    )
```

```python
import math

import jax
import jax.numpy as jnp
from jax import lax
from jax.experimental import pallas as pl
from jax.experimental.pallas import tpu as pltpu
from jax.sharding import PartitionSpec as P

LOSS_GAIN = 64.0
F32 = jnp.float32
BF16 = jnp.bfloat16
NN = (((1,), (0,)), ((), ()))
NT = (((1,), (1,)), ((), ()))
TN = (((0,), (0,)), ((), ()))
VMEM_LIMIT = 40 * 1024 * 1024
BACK_LIMIT = 24 * 1024 * 1024

REGIONS = 16
SEGS = 64
SEG_LEN = 32
CAP = 8
SLOTS = REGIONS * CAP
RAYS_DEV = 16
ROWS = SLOTS * SEG_LEN
ENC = 128
HID = 256
LAYERS = 4
BLOCK = 80

SIN = (3.141592588, -5.167707194, 2.550035118, -0.5980627511, 0.07724868669)
COS = (0.9999999532, -4.934792829, 4.058411309, -1.331876237, 0.219688854)


def iota(shape, axis):
    return lax.broadcasted_iota(jnp.int32, shape, axis)


def dot(a, b, dims=NN):
    return lax.dot_general(a, b, dims, preferred_element_type=F32)


def split3(x):
    hi = x.astype(BF16)
    rest = x - hi.astype(F32)
    mid = rest.astype(BF16)
    low = (rest - mid.astype(F32)).astype(BF16)
    return hi, mid, low


def pick(x, onehot, dims):
    hi, mid, low = split3(x)
    return dot(hi, onehot, dims) + (dot(mid, onehot, dims) + dot(low, onehot, dims))


def pick_left(onehot, x, dims):
    hi, mid, low = split3(x)
    return dot(onehot, hi, dims) + (dot(onehot, mid, dims) + dot(onehot, low, dims))


def as_mask(cond):
    return jnp.where(cond, 1.0, 0.0).astype(BF16)


def dispatch_kernel(pos_ref, sp_ref, tg_ref, seg_ref, send_ref, meta_ref):
    parity = lax.axis_index("region") % 2
    lane = iota((SEGS, SLOTS), 1)
    row = iota((SEGS, SEGS), 0)
    order = as_mask(iota((SEGS, SEGS), 1) == (row % RAYS_DEV) * 4 + row // RAYS_DEV)
    seg = dot(order, jnp.broadcast_to(seg_ref[...], (8, SEGS)).astype(F32).astype(BF16), NT)[:, 0:1]
    member = jnp.where(seg == lane.astype(F32), 1.0, 0.0)
    earlier = as_mask(iota((SEGS, SEGS), 1) < row)
    rank = dot(earlier, member.astype(BF16))
    slot = jnp.sum(member * (rank + (lane * CAP).astype(F32)), axis=1, keepdims=True)
    onehot = as_mask(slot == lane.astype(F32))
    parts = []
    for q in range(4):
        cut = slice(q * SEG_LEN, (q + 1) * SEG_LEN)
        parts.append(
            jnp.concatenate(
                [pos_ref[0, :, cut], pos_ref[1, :, cut], pos_ref[2, :, cut], sp_ref[:, cut]], axis=1
            )
        )
    data = jnp.concatenate(parts, axis=0)
    send_ref[...] = pick_left(onehot, data, TN)
    ids = dot(iota((8, SLOTS), 1).astype(BF16), onehot, NT)
    half = iota((8, 128), 1) // SEGS == parity
    ids = jnp.concatenate([ids, ids], axis=1)
    spread = as_mask(iota((RAYS_DEV, 128), 1) % RAYS_DEV == iota((RAYS_DEV, 128), 0))
    tg = pick(jnp.concatenate([tg_ref[...], tg_ref[...], tg_ref[0:2, :]], axis=0), spread, NN)
    meta_ref[...] = jnp.where(half, jnp.concatenate([ids[0:4], ids[0:1], tg[0:3]], axis=0), 0.0)


def dispatch(positions, spacing, targets, seg_region):
    return pl.pallas_call(
        dispatch_kernel,
        in_specs=[pl.BlockSpec(memory_space=pltpu.VMEM)] * 4,
        out_shape=(
            jax.ShapeDtypeStruct((SLOTS, 128), F32),
            pltpu.HBM((8, 128), F32),
        ),
        name="dispatch",
    )(positions, spacing, targets, seg_region)


def encode(pos, freq, first, count):
    cols = []
    for t in range(count):
        at = first + t
        cols.append(
            (freq[:, 0:1] * pos(0, at) + freq[:, 1:2] * pos(1, at)) + freq[:, 2:3] * pos(2, at)
        )
    turns = jnp.concatenate(cols, axis=1)
    x = turns - jnp.floor(turns + 0.5)
    y = x * x
    sine = x * (SIN[0] + y * (SIN[1] + y * (SIN[2] + y * (SIN[3] + y * SIN[4]))))
    cosine = COS[0] + y * (COS[1] + y * (COS[2] + y * (COS[3] + y * COS[4])))
    twice = sine + sine
    return jnp.concatenate([twice * cosine, 1.0 - twice * sine], axis=0).astype(BF16)


def local_render(raw, spacing):
    value = raw[0]
    small = jnp.exp(-jnp.abs(value))
    log1p = jnp.where(
        small < 0.02,
        small * (1.0 - small * (0.5 - small * (1.0 / 3.0 - small * 0.25))),
        jnp.log(1.0 + small),
    )
    density = jnp.maximum(value, 0.0) + log1p
    depth = density * spacing
    before = as_mask(iota((SEG_LEN, SEG_LEN), 1) < iota((SEG_LEN, SEG_LEN), 0))
    transmit = jnp.exp(-pick_left(before, depth, NN))
    fade = jnp.exp(-depth)
    opaque = jnp.where(
        depth < 0.03,
        depth * (1.0 - depth * (0.5 - depth * (1.0 / 6.0 - depth * (1.0 / 24.0)))),
        1.0 - fade,
    )
    weight = transmit * opaque
    tints = [0.5 + 0.5 * jnp.tanh(0.5 * raw[c]) for c in (1, 2, 3)]
    return depth, transmit, fade, weight, tints


def forward_kernel(
    recv_ref, meta_ref, freq_ref, win_ref, wh_ref, head_ref,
    send_ref, enc_ref, half_ref, local_ref,
    pos_ref, raw_ref, meta_copy, halves, encoded, local, send, sem, out_sem, *, chunk,
):
    meta = pltpu.make_async_copy(meta_ref, meta_copy, sem)
    meta.start()
    pos_ref[...] = jnp.transpose(recv_ref[...])
    count = chunk // SLOTS

    def pos(c, at):
        return pos_ref[c * SEG_LEN + at : c * SEG_LEN + at + 1, :]

    starts = range(0, ROWS, chunk)
    acts = []
    for start in starts:
        acts.append(encode(pos, freq_ref[...], start // SLOTS, count))
        encoded[:, start : start + chunk] = acts[-1]
    copies = [pltpu.make_async_copy(encoded, enc_ref, out_sem.at[LAYERS + 1])]
    copies[-1].start()
    for index in range(LAYERS + 1):
        weight = win_ref[...] if index == 0 else wh_ref[index - 1]
        for i, start in enumerate(starts):
            half = dot(weight, acts[i])
            acts[i] = (half + half * jnp.tanh(half)).astype(BF16)
            halves[index, :, start : start + chunk] = half.astype(BF16)
            if index == LAYERS:
                cut = pl.ds(start, chunk)
                at = out_sem.at[LAYERS + 3 + i] if i else out_sem.at[LAYERS]
                copies.append(pltpu.make_async_copy(halves.at[index, :, cut], half_ref.at[index, :, cut], at))
                copies[-1].start()
        if index < LAYERS:
            copies.append(pltpu.make_async_copy(halves.at[index], half_ref.at[index], out_sem.at[index]))
            copies[-1].start()
    for i, act in enumerate(acts):
        raw = dot(head_ref[...], act)
        for t in range(count):
            for c in range(4):
                raw_ref[c, i * count + t : i * count + t + 1, :] = raw[c : c + 1, t * SLOTS : (t + 1) * SLOTS]
    raw = [raw_ref[c] for c in range(4)]
    spacing = pos_ref[3 * SEG_LEN : 4 * SEG_LEN, :]
    depth, transmit, fade, weight, tints = local_render(raw, spacing)
    rows = [jnp.sum(depth, axis=0, keepdims=True)]
    rows += [jnp.sum(weight * tint, axis=0, keepdims=True) for tint in tints]
    meta.wait()
    block = jnp.concatenate(rows + [meta_copy[4:8, :]], axis=0)
    for r in range(REGIONS):
        send[r] = block
    copies.append(pltpu.make_async_copy(send, send_ref, out_sem.at[LAYERS + 3]))
    copies[-1].start()
    steep = (0.5 + 0.5 * jnp.tanh(0.5 * raw[0])) * spacing
    local[0] = transmit * fade * steep
    local[1] = steep
    for c in range(3):
        local[2 + c] = tints[c]
        local[5 + c] = weight * (tints[c] * (1.0 - tints[c]))
    local[8] = weight
    copies.append(pltpu.make_async_copy(local, local_ref, out_sem.at[LAYERS + 2]))
    copies[-1].start()
    for copy in copies:
        copy.wait()


def in_vmem(count):
    return [pl.BlockSpec(memory_space=pltpu.VMEM)] * count


def in_hbm(count):
    return [pl.BlockSpec(memory_space=pltpu.HBM)] * count


def forward_call(recv, meta, freq, win_t, wh_t, head, chunk=2048):
    kernel = lambda *refs: forward_kernel(*refs, chunk=chunk)
    specs = in_vmem(6)
    specs[1] = in_hbm(1)[0]
    meta = pltpu.with_memory_space_constraint(meta, pltpu.HBM)
    return pl.pallas_call(
        kernel,
        in_specs=specs,
        out_shape=(
            pltpu.HBM((REGIONS, 8, SLOTS), F32),
            pltpu.HBM((ENC, ROWS), BF16),
            pltpu.HBM((LAYERS + 1, HID, ROWS), BF16),
            pltpu.HBM((9, SEG_LEN, SLOTS), F32),
        ),
        out_specs=tuple(in_hbm(4)),
        scratch_shapes=[
            pltpu.VMEM((128, SLOTS), F32),
            pltpu.VMEM((4, SEG_LEN, SLOTS), F32),
            pltpu.VMEM((8, SLOTS), F32),
            pltpu.VMEM((LAYERS + 1, HID, ROWS), BF16),
            pltpu.VMEM((ENC, ROWS), BF16),
            pltpu.VMEM((9, SEG_LEN, SLOTS), F32),
            pltpu.VMEM((REGIONS, 8, SLOTS), F32),
            pltpu.SemaphoreType.DMA,
            pltpu.SemaphoreType.DMA((LAYERS + 3 + ROWS // chunk,)),
        ],
        compiler_params=pltpu.CompilerParams(vmem_limit_bytes=VMEM_LIMIT),
        cost_estimate=pl.CostEstimate(flops=2 * ROWS * 296000, bytes_accessed=700000, transcendentals=ROWS * 1280),
        name="forward",
    )(recv, meta, freq, win_t, wh_t, head)


def composite(me, got, gain):
    pairs = REGIONS // 2
    values = jnp.concatenate([got[r] for r in range(REGIONS)], axis=0)
    hi, mid, low = split3(values)
    lane = iota((1, 128), 1)
    sub = iota((128, 128), 0)
    depth_rows, colour_rows, target_rows, onehots = [], [[], [], []], [[], [], []], []
    for m in range(pairs):
        meta = got[2 * m, 4:8, :] + got[2 * m + 1, 4:8, :]
        ids = meta[0:1, :].astype(jnp.int32)
        owner = ids // CAP
        place = (2 * m + lane // SEGS) * CAP + ids % CAP
        onehot = sub == place
        picked = as_mask(onehot)
        found = dot(hi, picked) + (dot(mid, picked) + dot(low, picked))
        total = jnp.zeros((8, 128), F32)
        for r in range(REGIONS):
            total = total + jnp.where(owner == r, found[8 * r : 8 * r + 8], 0.0)
        depth_rows.append(total[0:1])
        for c in range(3):
            colour_rows[c].append(total[1 + c : 2 + c])
            target_rows[c].append(meta[1 + c : 2 + c])
        onehots.append(as_mask(jnp.logical_and(onehot, owner == me)))
    depth = jnp.concatenate(depth_rows, axis=0)
    colours = [jnp.concatenate(rows, axis=0) for rows in colour_rows]
    targets = [jnp.concatenate(rows, axis=0) for rows in target_rows]
    within = iota((pairs, 128), 1) % SEGS

    def earlier(x):
        total = jnp.zeros_like(x)
        for k in (1, 2, 3):
            total = total + jnp.where(within >= k * RAYS_DEV, pltpu.roll(x, k * RAYS_DEV, 1), 0.0)
        return total

    def later(x):
        total = jnp.zeros_like(x)
        for k in (1, 2, 3):
            total = total + jnp.where(within < SEGS - k * RAYS_DEV, pltpu.roll(x, 128 - k * RAYS_DEV, 1), 0.0)
        return total

    transmit = jnp.exp(-earlier(depth))
    behind = jnp.zeros((pairs, 128), F32)
    pixels, scaled = [], []
    for c in range(3):
        weighted = transmit * colours[c]
        after = later(weighted)
        pixel = (earlier(weighted) + weighted) + after
        pull = (pixel - targets[c]) * gain
        behind = behind + pull * after
        scaled.append(transmit * pull)
        pixels.append(pixel)
    rows = scaled + [behind]
    slots = jnp.zeros((32, SLOTS), F32)
    for m in range(pairs):
        x = jnp.concatenate([r[m : m + 1] for r in rows] + [jnp.zeros((4, 128), F32)], axis=0)
        parts = jnp.concatenate([p.astype(F32) for p in split3(x)] + [jnp.zeros((8, 128), F32)], axis=0)
        slots = slots + dot(parts.astype(BF16), onehots[m], NT)
    slots = slots[0:8] + (slots[8:16] + slots[16:24])
    own = []
    mine = jnp.logical_and(iota((pairs, 128), 0) == me // 2, iota((pairs, 128), 1) // SEGS == me % 2)
    for c in range(3):
        row = jnp.sum(jnp.where(mine, pixels[c], 0.0), axis=0, keepdims=True)
        own.append((row + pltpu.roll(row, SEGS, 1))[:, 0:RAYS_DEV])
    return slots, jnp.concatenate(own, axis=0)


def residual_of(half):
    tanh = jnp.tanh(half)
    above = 1.0 + tanh
    return half * above, above + half * (above * (1.0 - tanh))


def fetch_kernel(local_in, half_in, local_ref, top_ref, sem):
    copies = [
        pltpu.make_async_copy(half_in.at[LAYERS], top_ref, sem.at[0]),
        pltpu.make_async_copy(local_in, local_ref, sem.at[1]),
    ]
    for copy in copies:
        copy.start()
    for copy in copies:
        copy.wait()


def fetch_call(local, half):
    return pl.pallas_call(
        fetch_kernel,
        in_specs=in_hbm(2),
        out_specs=tuple(in_vmem(2)),
        out_shape=(
            jax.ShapeDtypeStruct((9, SEG_LEN, SLOTS), F32),
            jax.ShapeDtypeStruct((HID, ROWS), BF16),
        ),
        scratch_shapes=[pltpu.SemaphoreType.DMA((2,))],
        compiler_params=pltpu.CompilerParams(vmem_limit_bytes=16 * 1024 * 1024),
        cost_estimate=pl.CostEstimate(flops=2 * 10**9, bytes_accessed=2 * 10**7, transcendentals=0),
        name="fetch",
    )(*[pltpu.with_memory_space_constraint(x, pltpu.HBM) for x in (local, half)])


def backward_kernel(
    got_ref, wh_ref, head_ref, local_ref, top_ref, enc_in, half_in,
    pix_ref, keep_ref, send_ref, up_ref, gin_ref, gh_ref, halves, enc_ref, in_sem, *, chunk, gain,
):
    copies = [
        pltpu.make_async_copy(half_in.at[index], halves.at[index], in_sem.at[index]) for index in range(LAYERS)
    ]
    copies.append(pltpu.make_async_copy(enc_in, enc_ref, in_sem.at[LAYERS]))
    for copy in copies[LAYERS - 1 :: -1] + copies[LAYERS:]:
        copy.start()
    slots, pixel = composite(lax.axis_index("region"), got_ref, gain)
    pix_ref[...] = pixel
    pull = jnp.zeros((SEG_LEN, SLOTS), F32)
    for c in range(3):
        pull = pull + slots[c : c + 1] * local_ref[2 + c]
    after = as_mask(iota((SEG_LEN, SEG_LEN), 1) > iota((SEG_LEN, SEG_LEN), 0))
    rest = pick_left(after, local_ref[8] * pull, NN) + slots[3:4]
    ups = [local_ref[0] * pull - rest * local_ref[1]]
    ups += [slots[c : c + 1] * local_ref[5 + c] for c in range(3)]
    up_ref[...] = jnp.zeros_like(up_ref)
    for c in range(4):
        for t in range(SEG_LEN):
            up_ref[c : c + 1, t * SLOTS : (t + 1) * SLOTS] = ups[c][t : t + 1]

    cuts = [slice(start, start + chunk) for start in range(0, ROWS, chunk)]

    def residual(index, cut):
        half = top_ref[:, cut] if index == LAYERS else halves[index, :, cut]
        return residual_of(half)

    flows, slopes = [], []
    ghead = jnp.zeros((8, HID), F32)
    for cut in cuts:
        up = up_ref[:, cut].astype(BF16)
        flows.append(dot(head_ref[...], up))
        act, slope = residual(LAYERS, cut)
        slopes.append(slope)
        ghead = ghead + dot(up, act, NT)
    for index in range(LAYERS, -1, -1):
        for copy in {LAYERS: copies[LAYERS - 1 : LAYERS], LAYERS - 1: copies[1 : LAYERS - 1], 1: [copies[0], copies[LAYERS]]}.get(index, []):
            copy.wait()
        total = None
        for i, cut in enumerate(cuts):
            back = flows[i].astype(BF16) * slopes[i]
            if index > 0:
                flows[i] = dot(wh_ref[index - 1], back)
                act, slopes[i] = residual(index - 1, cut)
            else:
                act = enc_ref[:, cut]
            part = dot(act, back, NT)
            total = part if total is None else total + part
        if index > 0:
            gh_ref[index - 1] = total
        else:
            gin_ref[...] = total
    core = lax.axis_index("dp") % 2
    for ref, which in ((keep_ref, core), (send_ref, 1 - core)):
        for z in range(8):
            to = z * 2 + which
            for l in range(LAYERS):
                rows = gh_ref[l, pl.ds(pl.multiple_of(to * 16, 16), 16), :]
                ref[z, l * 16 : (l + 1) * 16, :] = rows.astype(BF16)
            rows = gin_ref[pl.ds(pl.multiple_of(to * 8, 8), 8), :]
            ref[z, 64:80, :] = jnp.concatenate([rows, ghead], axis=0).astype(BF16)


def backward_call(got, wh, head, local, top, enc, half, gain, chunk=512):
    enc, half = [pltpu.with_memory_space_constraint(x, pltpu.HBM) for x in (enc, half)]
    kernel = lambda *refs: backward_kernel(*refs, chunk=chunk, gain=gain)
    return pl.pallas_call(
        kernel,
        in_specs=in_vmem(5) + in_hbm(2),
        out_shape=(
            jax.ShapeDtypeStruct((3, RAYS_DEV), F32),
            jax.ShapeDtypeStruct((8, BLOCK, HID), BF16),
            jax.ShapeDtypeStruct((8, BLOCK, HID), BF16),
        ),
        scratch_shapes=[
            pltpu.VMEM((8, ROWS), F32),
            pltpu.VMEM((ENC, HID), F32),
            pltpu.VMEM((LAYERS, HID, HID), F32),
            pltpu.VMEM((LAYERS, HID, ROWS), BF16),
            pltpu.VMEM((ENC, ROWS), BF16),
            pltpu.SemaphoreType.DMA((LAYERS + 1,)),
        ],
        compiler_params=pltpu.CompilerParams(vmem_limit_bytes=BACK_LIMIT),
        cost_estimate=pl.CostEstimate(flops=4 * ROWS * 296000, bytes_accessed=23000000, transcendentals=0),
        name="backward",
    )(got, wh, head, local, top, enc, half)


def total_kernel(got_ref, gin_ref, gh_ref, ghead_ref):
    total = got_ref[0].astype(F32)
    for z in range(1, 8):
        total = total + got_ref[z].astype(F32)
    for l in range(LAYERS):
        gh_ref[0, l] = total[l * 16 : (l + 1) * 16]
    gin_ref[0] = total[64:72]
    mine = iota((HID, 16), 0) == lax.axis_index("dp") * 16 + iota((HID, 16), 1)
    ghead_ref[0] = pick(total[72:80], as_mask(mine), NN)[0:4]


def total_call(got):
    return pl.pallas_call(
        total_kernel,
        in_specs=in_vmem(1),
        out_shape=(
            jax.ShapeDtypeStruct((1, 8, HID), F32),
            jax.ShapeDtypeStruct((1, LAYERS, 16, HID), F32),
            jax.ShapeDtypeStruct((1, 4, 16), F32),
        ),
        name="total",
    )(got)


def per_device(positions, spacing, targets, frequencies, seg_region, w_in, w_hidden, w_head):
    rays = spacing.shape[0] * lax.axis_size("region") * lax.axis_size("dp")
    gain = LOSS_GAIN / math.sqrt(rays)

    half = jnp.asarray(0.5, BF16)
    win_t = w_in[0].T * half
    wh_t = jnp.transpose(w_hidden[0], (0, 2, 1)) * half
    wh_half = w_hidden[0] * half
    head = w_head[0]
    head_t = jnp.pad(head, ((0, 4), (0, 0))).T * half
    freq = frequencies.T

    outgoing, meta = dispatch(positions, spacing, targets, seg_region.reshape(1, SEGS))
    arrived = lax.all_to_all(
        outgoing.reshape(REGIONS, CAP, 128), "region", split_axis=0, concat_axis=0, tiled=True
    ).reshape(SLOTS, 128)
    summary, enc, half_pre, local = forward_call(arrived, meta, freq, win_t, wh_t, head)
    got = lax.all_to_all(summary, "region", split_axis=0, concat_axis=0, tiled=True)
    local, top = fetch_call(local, half_pre)
    pixel_color, keep, send = backward_call(got, wh_half, head_t, local, top, enc, half_pre, gain)
    other = lax.ppermute(send, "dp", [(i, i ^ 1) for i in range(16)])
    both = (keep.astype(F32) + other.astype(F32)).astype(BF16)
    groups = [list(range(0, 16, 2)), list(range(1, 16, 2))]
    parts = lax.all_to_all(both, "dp", 0, 0, tiled=True, axis_index_groups=groups)
    grad_in, grad_hidden, grad_head = total_call(parts)
    return pixel_color, grad_in, grad_hidden, grad_head


def solution(mesh):
    return jax.shard_map(
        per_device,
        mesh=mesh,
        in_specs=(
            P(None, ("region", "dp"), None),
            P(("region", "dp"), None),
            P(None, ("region", "dp")),
            P(),
            P(("region", "dp"), None),
            P("region", None, None),
            P("region", None, None, None),
            P("region", None, None),
        ),
        out_specs=(
            P(None, ("region", "dp")),
            P("region", "dp", None),
            P("region", None, "dp", None),
            P("region", None, "dp"),
        ),
        check_vma=False,
    )
```

```python
import math

import jax
import jax.numpy as jnp
from jax import lax
from jax.experimental import pallas as pl
from jax.experimental.pallas import tpu as pltpu
from jax.sharding import PartitionSpec as P

LOSS_GAIN = 64.0
F32 = jnp.float32
BF16 = jnp.bfloat16
NN = (((1,), (0,)), ((), ()))
NT = (((1,), (1,)), ((), ()))
VMEM_LIMIT = 40 * 1024 * 1024
BACK_LIMIT = 24 * 1024 * 1024

REGIONS = 16
SEGS = 64
SEG_LEN = 32
CAP = 8
SLOTS = REGIONS * CAP
RAYS_DEV = 16
ROWS = SLOTS * SEG_LEN
ENC = 128
HID = 256
LAYERS = 4
BLOCK = 80

SIN = (3.141592588, -5.167707194, 2.550035118, -0.5980627511, 0.07724868669)
COS = (0.9999999532, -4.934792829, 4.058411309, -1.331876237, 0.219688854)


def iota(shape, axis):
    return lax.broadcasted_iota(jnp.int32, shape, axis)


def dot(a, b, dims=NN):
    return lax.dot_general(a, b, dims, preferred_element_type=F32)


def split3(x):
    hi = x.astype(BF16)
    rest = x - hi.astype(F32)
    mid = rest.astype(BF16)
    low = (rest - mid.astype(F32)).astype(BF16)
    return hi, mid, low


def pick(x, onehot, dims):
    hi, mid, low = split3(x)
    return dot(hi, onehot, dims) + (dot(mid, onehot, dims) + dot(low, onehot, dims))


def pick_left(onehot, x, dims):
    hi, mid, low = split3(x)
    return dot(onehot, hi, dims) + (dot(onehot, mid, dims) + dot(onehot, low, dims))


def as_mask(cond):
    return jnp.where(cond, 1.0, 0.0).astype(BF16)


def dispatch_kernel(pos_ref, sp_ref, tg_ref, seg_ref, send_ref, meta_ref):
    parity = lax.axis_index("region") % 2
    at = iota((SEGS, SEGS), 1)
    order = as_mask(iota((SEGS, SEGS), 0) == (at % RAYS_DEV) * 4 + at // RAYS_DEV)
    seg = dot(jnp.broadcast_to(seg_ref[...], (REGIONS, SEGS)).astype(F32).astype(BF16), order)
    region = iota((REGIONS, SEGS), 0).astype(F32)
    member = seg == region
    rank = dot(as_mask(member), as_mask(iota((SEGS, SEGS), 0) < at))
    slot = jnp.sum(jnp.where(member, rank + region * CAP, 0.0), axis=0, keepdims=True)
    onehot = as_mask(iota((SLOTS, SEGS), 0).astype(F32) == slot)
    parts = []
    for q in range(4):
        cut = slice(q * SEG_LEN, (q + 1) * SEG_LEN)
        parts.append(
            jnp.concatenate(
                [pos_ref[0, :, cut], pos_ref[1, :, cut], pos_ref[2, :, cut], sp_ref[:, cut]], axis=1
            )
        )
    data = jnp.concatenate(parts, axis=0)
    send_ref[...] = pick_left(onehot, data, NN)
    half = iota((8, 128), 1) // SEGS == parity
    ids = jnp.broadcast_to(jnp.concatenate([slot, slot], axis=1), (5, 128))
    spread = as_mask(iota((RAYS_DEV, 128), 1) % RAYS_DEV == iota((RAYS_DEV, 128), 0))
    tg = pick(jnp.concatenate([tg_ref[...], tg_ref[...], tg_ref[0:2, :]], axis=0), spread, NN)
    meta_ref[...] = jnp.where(half, jnp.concatenate([ids, tg[0:3]], axis=0), 0.0)


def dispatch(positions, spacing, targets, seg_region):
    return pl.pallas_call(
        dispatch_kernel,
        in_specs=[pl.BlockSpec(memory_space=pltpu.VMEM)] * 4,
        out_shape=(
            jax.ShapeDtypeStruct((SLOTS, 128), F32),
            pltpu.HBM((8, 128), F32),
        ),
        name="dispatch",
    )(positions, spacing, targets, seg_region)


def encode(pos, freq, first, count):
    cols = []
    for t in range(count):
        at = first + t
        cols.append(
            (freq[:, 0:1] * pos(0, at) + freq[:, 1:2] * pos(1, at)) + freq[:, 2:3] * pos(2, at)
        )
    turns = jnp.concatenate(cols, axis=1)
    x = turns - jnp.floor(turns + 0.5)
    y = x * x
    sine = x * (SIN[0] + y * (SIN[1] + y * (SIN[2] + y * (SIN[3] + y * SIN[4]))))
    cosine = COS[0] + y * (COS[1] + y * (COS[2] + y * (COS[3] + y * COS[4])))
    twice = sine + sine
    return jnp.concatenate([twice * cosine, 1.0 - twice * sine], axis=0).astype(BF16)


def local_render(raw, spacing):
    value = raw[0]
    small = jnp.exp(-jnp.abs(value))
    log1p = jnp.where(
        small < 0.02,
        small * (1.0 - small * (0.5 - small * (1.0 / 3.0 - small * 0.25))),
        jnp.log(1.0 + small),
    )
    density = jnp.maximum(value, 0.0) + log1p
    depth = density * spacing
    before = as_mask(iota((SEG_LEN, SEG_LEN), 1) < iota((SEG_LEN, SEG_LEN), 0))
    transmit = jnp.exp(-pick_left(before, depth, NN))
    fade = jnp.exp(-depth)
    opaque = jnp.where(
        depth < 0.03,
        depth * (1.0 - depth * (0.5 - depth * (1.0 / 6.0 - depth * (1.0 / 24.0)))),
        1.0 - fade,
    )
    weight = transmit * opaque
    tints = [0.5 + 0.5 * jnp.tanh(0.5 * raw[c]) for c in (1, 2, 3)]
    return depth, transmit, fade, weight, tints


def forward_kernel(
    recv_ref, meta_ref, freq_ref, win_ref, wh_ref, head_ref,
    send_ref, enc_ref, half_ref, local_ref,
    pos_ref, raw_ref, meta_copy, halves, encoded, local, send, sem, out_sem, *, chunk,
):
    meta = pltpu.make_async_copy(meta_ref, meta_copy, sem)
    meta.start()
    pos_ref[...] = jnp.transpose(recv_ref[...])
    count = chunk // SLOTS

    def pos(c, at):
        return pos_ref[c * SEG_LEN + at : c * SEG_LEN + at + 1, :]

    starts = range(0, ROWS, chunk)
    acts = []
    for start in starts:
        acts.append(encode(pos, freq_ref[...], start // SLOTS, count))
        encoded[:, start : start + chunk] = acts[-1]
    copies = [pltpu.make_async_copy(encoded, enc_ref, out_sem.at[LAYERS + 1])]
    copies[-1].start()
    for index in range(LAYERS + 1):
        weight = win_ref[...] if index == 0 else wh_ref[index - 1]
        for i, start in enumerate(starts):
            half = dot(weight, acts[i])
            acts[i] = (half + half * jnp.tanh(half)).astype(BF16)
            halves[index, :, start : start + chunk] = half.astype(BF16)
            if index == LAYERS:
                cut = pl.ds(start, chunk)
                at = out_sem.at[LAYERS + 3 + i] if i else out_sem.at[LAYERS]
                copies.append(pltpu.make_async_copy(halves.at[index, :, cut], half_ref.at[index, :, cut], at))
                copies[-1].start()
        if index < LAYERS:
            copies.append(pltpu.make_async_copy(halves.at[index], half_ref.at[index], out_sem.at[index]))
            copies[-1].start()
    for i, act in enumerate(acts):
        raw = dot(head_ref[...], act)
        for t in range(count):
            for c in range(4):
                raw_ref[c, i * count + t : i * count + t + 1, :] = raw[c : c + 1, t * SLOTS : (t + 1) * SLOTS]
    raw = [raw_ref[c] for c in range(4)]
    spacing = pos_ref[3 * SEG_LEN : 4 * SEG_LEN, :]
    depth, transmit, fade, weight, tints = local_render(raw, spacing)
    rows = [jnp.sum(depth, axis=0, keepdims=True)]
    rows += [jnp.sum(weight * tint, axis=0, keepdims=True) for tint in tints]
    meta.wait()
    block = jnp.concatenate(rows + [meta_copy[4:8, :]], axis=0)
    for r in range(REGIONS):
        send[r] = block
    copies.append(pltpu.make_async_copy(send, send_ref, out_sem.at[LAYERS + 3]))
    copies[-1].start()
    steep = (0.5 + 0.5 * jnp.tanh(0.5 * raw[0])) * spacing
    local[0] = transmit * fade * steep
    local[1] = steep
    for c in range(3):
        local[2 + c] = tints[c]
        local[5 + c] = weight * (tints[c] * (1.0 - tints[c]))
    local[8] = weight
    copies.append(pltpu.make_async_copy(local, local_ref, out_sem.at[LAYERS + 2]))
    copies[-1].start()
    for copy in copies:
        copy.wait()


def in_vmem(count):
    return [pl.BlockSpec(memory_space=pltpu.VMEM)] * count


def in_hbm(count):
    return [pl.BlockSpec(memory_space=pltpu.HBM)] * count


def forward_call(recv, meta, freq, win_t, wh_t, head, chunk=2048):
    kernel = lambda *refs: forward_kernel(*refs, chunk=chunk)
    specs = in_vmem(6)
    specs[1] = in_hbm(1)[0]
    meta = pltpu.with_memory_space_constraint(meta, pltpu.HBM)
    return pl.pallas_call(
        kernel,
        in_specs=specs,
        out_shape=(
            pltpu.HBM((REGIONS, 8, SLOTS), F32),
            pltpu.HBM((ENC, ROWS), BF16),
            pltpu.HBM((LAYERS + 1, HID, ROWS), BF16),
            pltpu.HBM((9, SEG_LEN, SLOTS), F32),
        ),
        out_specs=tuple(in_hbm(4)),
        scratch_shapes=[
            pltpu.VMEM((128, SLOTS), F32),
            pltpu.VMEM((4, SEG_LEN, SLOTS), F32),
            pltpu.VMEM((8, SLOTS), F32),
            pltpu.VMEM((LAYERS + 1, HID, ROWS), BF16),
            pltpu.VMEM((ENC, ROWS), BF16),
            pltpu.VMEM((9, SEG_LEN, SLOTS), F32),
            pltpu.VMEM((REGIONS, 8, SLOTS), F32),
            pltpu.SemaphoreType.DMA,
            pltpu.SemaphoreType.DMA((LAYERS + 3 + ROWS // chunk,)),
        ],
        compiler_params=pltpu.CompilerParams(vmem_limit_bytes=VMEM_LIMIT),
        cost_estimate=pl.CostEstimate(flops=2 * ROWS * 296000, bytes_accessed=700000, transcendentals=ROWS * 1280),
        name="forward",
    )(recv, meta, freq, win_t, wh_t, head)


def composite(me, got, gain):
    pairs = REGIONS // 2
    values = jnp.concatenate([got[r] for r in range(REGIONS)], axis=0)
    hi, mid, low = split3(values)
    lane = iota((1, 128), 1)
    sub = iota((128, 128), 0)
    depth_rows, colour_rows, target_rows, onehots = [], [[], [], []], [[], [], []], []
    for m in range(pairs):
        meta = got[2 * m, 4:8, :] + got[2 * m + 1, 4:8, :]
        ids = meta[0:1, :].astype(jnp.int32)
        owner = ids // CAP
        place = (2 * m + lane // SEGS) * CAP + ids % CAP
        onehot = sub == place
        picked = as_mask(onehot)
        found = dot(hi, picked) + (dot(mid, picked) + dot(low, picked))
        total = jnp.zeros((8, 128), F32)
        for r in range(REGIONS):
            total = total + jnp.where(owner == r, found[8 * r : 8 * r + 8], 0.0)
        depth_rows.append(total[0:1])
        for c in range(3):
            colour_rows[c].append(total[1 + c : 2 + c])
            target_rows[c].append(meta[1 + c : 2 + c])
        onehots.append(as_mask(jnp.logical_and(onehot, owner == me)))
    depth = jnp.concatenate(depth_rows, axis=0)
    colours = [jnp.concatenate(rows, axis=0) for rows in colour_rows]
    targets = [jnp.concatenate(rows, axis=0) for rows in target_rows]
    within = iota((pairs, 128), 1) % SEGS

    def earlier(x):
        total = jnp.zeros_like(x)
        for k in (1, 2, 3):
            total = total + jnp.where(within >= k * RAYS_DEV, pltpu.roll(x, k * RAYS_DEV, 1), 0.0)
        return total

    def later(x):
        total = jnp.zeros_like(x)
        for k in (1, 2, 3):
            total = total + jnp.where(within < SEGS - k * RAYS_DEV, pltpu.roll(x, 128 - k * RAYS_DEV, 1), 0.0)
        return total

    transmit = jnp.exp(-earlier(depth))
    behind = jnp.zeros((pairs, 128), F32)
    pixels, scaled = [], []
    for c in range(3):
        weighted = transmit * colours[c]
        after = later(weighted)
        pixel = (earlier(weighted) + weighted) + after
        pull = (pixel - targets[c]) * gain
        behind = behind + pull * after
        scaled.append(transmit * pull)
        pixels.append(pixel)
    rows = scaled + [behind]
    slots = jnp.zeros((32, SLOTS), F32)
    for m in range(pairs):
        x = jnp.concatenate([r[m : m + 1] for r in rows] + [jnp.zeros((4, 128), F32)], axis=0)
        parts = jnp.concatenate([p.astype(F32) for p in split3(x)] + [jnp.zeros((8, 128), F32)], axis=0)
        slots = slots + dot(parts.astype(BF16), onehots[m], NT)
    slots = slots[0:8] + (slots[8:16] + slots[16:24])
    own = []
    mine = jnp.logical_and(iota((pairs, 128), 0) == me // 2, iota((pairs, 128), 1) // SEGS == me % 2)
    for c in range(3):
        row = jnp.sum(jnp.where(mine, pixels[c], 0.0), axis=0, keepdims=True)
        own.append((row + pltpu.roll(row, SEGS, 1))[:, 0:RAYS_DEV])
    return slots, jnp.concatenate(own, axis=0)


def residual_of(half):
    tanh = jnp.tanh(half)
    above = 1.0 + tanh
    return half * above, above + half * (above * (1.0 - tanh))


def fetch_kernel(local_in, half_in, local_ref, top_ref, sem):
    copies = [
        pltpu.make_async_copy(half_in.at[LAYERS], top_ref, sem.at[0]),
        pltpu.make_async_copy(local_in, local_ref, sem.at[1]),
    ]
    for copy in copies:
        copy.start()
    for copy in copies:
        copy.wait()


def fetch_call(local, half):
    return pl.pallas_call(
        fetch_kernel,
        in_specs=in_hbm(2),
        out_specs=tuple(in_vmem(2)),
        out_shape=(
            jax.ShapeDtypeStruct((9, SEG_LEN, SLOTS), F32),
            jax.ShapeDtypeStruct((HID, ROWS), BF16),
        ),
        scratch_shapes=[pltpu.SemaphoreType.DMA((2,))],
        compiler_params=pltpu.CompilerParams(vmem_limit_bytes=16 * 1024 * 1024),
        cost_estimate=pl.CostEstimate(flops=2 * 10**9, bytes_accessed=2 * 10**7, transcendentals=0),
        name="fetch",
    )(*[pltpu.with_memory_space_constraint(x, pltpu.HBM) for x in (local, half)])


def backward_kernel(
    got_ref, wh_ref, head_ref, local_ref, top_ref, enc_in, half_in,
    pix_ref, keep_ref, send_ref, up_ref, gin_ref, gh_ref, halves, enc_ref, in_sem, *, chunk, gain,
):
    copies = [
        pltpu.make_async_copy(half_in.at[index], halves.at[index], in_sem.at[index]) for index in range(LAYERS)
    ]
    copies.append(pltpu.make_async_copy(enc_in, enc_ref, in_sem.at[LAYERS]))
    for copy in copies[LAYERS - 1 :: -1] + copies[LAYERS:]:
        copy.start()
    slots, pixel = composite(lax.axis_index("region"), got_ref, gain)
    pix_ref[...] = pixel
    pull = jnp.zeros((SEG_LEN, SLOTS), F32)
    for c in range(3):
        pull = pull + slots[c : c + 1] * local_ref[2 + c]
    after = as_mask(iota((SEG_LEN, SEG_LEN), 1) > iota((SEG_LEN, SEG_LEN), 0))
    rest = pick_left(after, local_ref[8] * pull, NN) + slots[3:4]
    ups = [local_ref[0] * pull - rest * local_ref[1]]
    ups += [slots[c : c + 1] * local_ref[5 + c] for c in range(3)]
    up_ref[...] = jnp.zeros_like(up_ref)
    for c in range(4):
        for t in range(SEG_LEN):
            up_ref[c : c + 1, t * SLOTS : (t + 1) * SLOTS] = ups[c][t : t + 1]

    cuts = [slice(start, start + chunk) for start in range(0, ROWS, chunk)]

    def residual(index, cut):
        half = top_ref[:, cut] if index == LAYERS else halves[index, :, cut]
        return residual_of(half)

    flows, slopes = [], []
    ghead = jnp.zeros((8, HID), F32)
    for cut in cuts:
        up = up_ref[:, cut].astype(BF16)
        flows.append(dot(head_ref[...], up))
        act, slope = residual(LAYERS, cut)
        slopes.append(slope)
        ghead = ghead + dot(up, act, NT)
    for index in range(LAYERS, -1, -1):
        for copy in {LAYERS: copies[LAYERS - 1 : LAYERS], LAYERS - 1: copies[1 : LAYERS - 1], 1: [copies[0], copies[LAYERS]]}.get(index, []):
            copy.wait()
        total = None
        for i, cut in enumerate(cuts):
            back = flows[i].astype(BF16) * slopes[i]
            if index > 0:
                flows[i] = dot(wh_ref[index - 1], back)
                act, slopes[i] = residual(index - 1, cut)
            else:
                act = enc_ref[:, cut]
            part = dot(act, back, NT)
            total = part if total is None else total + part
        if index > 0:
            gh_ref[index - 1] = total
        else:
            gin_ref[...] = total
    core = lax.axis_index("dp") % 2
    for ref, which in ((keep_ref, core), (send_ref, 1 - core)):
        for z in range(8):
            to = z * 2 + which
            for l in range(LAYERS):
                rows = gh_ref[l, pl.ds(pl.multiple_of(to * 16, 16), 16), :]
                ref[z, l * 16 : (l + 1) * 16, :] = rows.astype(BF16)
            rows = gin_ref[pl.ds(pl.multiple_of(to * 8, 8), 8), :]
            ref[z, 64:80, :] = jnp.concatenate([rows, ghead], axis=0).astype(BF16)


def backward_call(got, wh, head, local, top, enc, half, gain, chunk=512):
    enc, half = [pltpu.with_memory_space_constraint(x, pltpu.HBM) for x in (enc, half)]
    kernel = lambda *refs: backward_kernel(*refs, chunk=chunk, gain=gain)
    return pl.pallas_call(
        kernel,
        in_specs=in_vmem(5) + in_hbm(2),
        out_shape=(
            jax.ShapeDtypeStruct((3, RAYS_DEV), F32),
            jax.ShapeDtypeStruct((8, BLOCK, HID), BF16),
            jax.ShapeDtypeStruct((8, BLOCK, HID), BF16),
        ),
        scratch_shapes=[
            pltpu.VMEM((8, ROWS), F32),
            pltpu.VMEM((ENC, HID), F32),
            pltpu.VMEM((LAYERS, HID, HID), F32),
            pltpu.VMEM((LAYERS, HID, ROWS), BF16),
            pltpu.VMEM((ENC, ROWS), BF16),
            pltpu.SemaphoreType.DMA((LAYERS + 1,)),
        ],
        compiler_params=pltpu.CompilerParams(vmem_limit_bytes=BACK_LIMIT),
        cost_estimate=pl.CostEstimate(flops=4 * ROWS * 296000, bytes_accessed=23000000, transcendentals=0),
        name="backward",
    )(got, wh, head, local, top, enc, half)


def total_kernel(got_ref, gin_ref, gh_ref, ghead_ref):
    total = got_ref[0].astype(F32)
    for z in range(1, 8):
        total = total + got_ref[z].astype(F32)
    for l in range(LAYERS):
        gh_ref[0, l] = total[l * 16 : (l + 1) * 16]
    gin_ref[0] = total[64:72]
    mine = iota((HID, 16), 0) == lax.axis_index("dp") * 16 + iota((HID, 16), 1)
    ghead_ref[0] = pick(total[72:80], as_mask(mine), NN)[0:4]


def total_call(got):
    return pl.pallas_call(
        total_kernel,
        in_specs=in_vmem(1),
        out_shape=(
            jax.ShapeDtypeStruct((1, 8, HID), F32),
            jax.ShapeDtypeStruct((1, LAYERS, 16, HID), F32),
            jax.ShapeDtypeStruct((1, 4, 16), F32),
        ),
        name="total",
    )(got)


def per_device(positions, spacing, targets, frequencies, seg_region, w_in, w_hidden, w_head):
    rays = spacing.shape[0] * lax.axis_size("region") * lax.axis_size("dp")
    gain = LOSS_GAIN / math.sqrt(rays)

    half = jnp.asarray(0.5, BF16)
    win_t = w_in[0].T * half
    wh_t = jnp.transpose(w_hidden[0], (0, 2, 1)) * half
    wh_half = w_hidden[0] * half
    head = w_head[0]
    head_t = jnp.pad(head, ((0, 4), (0, 0))).T * half
    freq = frequencies.T

    outgoing, meta = dispatch(positions, spacing, targets, seg_region.reshape(1, SEGS))
    arrived = lax.all_to_all(
        outgoing.reshape(REGIONS, CAP, 128), "region", split_axis=0, concat_axis=0, tiled=True
    ).reshape(SLOTS, 128)
    summary, enc, half_pre, local = forward_call(arrived, meta, freq, win_t, wh_t, head)
    got = lax.all_to_all(summary, "region", split_axis=0, concat_axis=0, tiled=True)
    local, top = fetch_call(local, half_pre)
    pixel_color, keep, send = backward_call(got, wh_half, head_t, local, top, enc, half_pre, gain)
    other = lax.ppermute(send, "dp", [(i, i ^ 1) for i in range(16)])
    both = (keep.astype(F32) + other.astype(F32)).astype(BF16)
    groups = [list(range(0, 16, 2)), list(range(1, 16, 2))]
    parts = lax.all_to_all(both, "dp", 0, 0, tiled=True, axis_index_groups=groups)
    grad_in, grad_hidden, grad_head = total_call(parts)
    return pixel_color, grad_in, grad_hidden, grad_head


def solution(mesh):
    return jax.shard_map(
        per_device,
        mesh=mesh,
        in_specs=(
            P(None, ("region", "dp"), None),
            P(("region", "dp"), None),
            P(None, ("region", "dp")),
            P(),
            P(("region", "dp"), None),
            P("region", None, None),
            P("region", None, None, None),
            P("region", None, None),
        ),
        out_specs=(
            P(None, ("region", "dp")),
            P("region", "dp", None),
            P("region", None, "dp", None),
            P("region", None, "dp"),
        ),
        check_vma=False,
    )
```

```python
import math

import jax
import jax.numpy as jnp
from jax import lax
from jax.experimental import pallas as pl
from jax.experimental.pallas import tpu as pltpu
from jax.sharding import PartitionSpec as P

LOSS_GAIN = 64.0
F32 = jnp.float32
BF16 = jnp.bfloat16
NN = (((1,), (0,)), ((), ()))
NT = (((1,), (1,)), ((), ()))
VMEM_LIMIT = 40 * 1024 * 1024
BACK_LIMIT = 24 * 1024 * 1024

REGIONS = 16
SEGS = 64
SEG_LEN = 32
CAP = 8
SLOTS = REGIONS * CAP
RAYS_DEV = 16
ROWS = SLOTS * SEG_LEN
ENC = 128
HID = 256
LAYERS = 4
BLOCK = 80

SIN = (3.141592588, -5.167707194, 2.550035118, -0.5980627511, 0.07724868669)
COS = (0.9999999532, -4.934792829, 4.058411309, -1.331876237, 0.219688854)


def iota(shape, axis):
    return lax.broadcasted_iota(jnp.int32, shape, axis)


def dot(a, b, dims=NN):
    return lax.dot_general(a, b, dims, preferred_element_type=F32)


def split3(x):
    hi = x.astype(BF16)
    rest = x - hi.astype(F32)
    mid = rest.astype(BF16)
    low = (rest - mid.astype(F32)).astype(BF16)
    return hi, mid, low


def pick(x, onehot, dims):
    hi, mid, low = split3(x)
    return dot(hi, onehot, dims) + (dot(mid, onehot, dims) + dot(low, onehot, dims))


def pick_left(onehot, x, dims):
    hi, mid, low = split3(x)
    return dot(onehot, hi, dims) + (dot(onehot, mid, dims) + dot(onehot, low, dims))


def as_mask(cond):
    return jnp.where(cond, 1.0, 0.0).astype(BF16)


def dispatch_kernel(pos_ref, sp_ref, tg_ref, seg_ref, send_ref, meta_ref):
    parity = lax.axis_index("region") % 2
    at = iota((SEGS, SEGS), 1)
    order = as_mask(iota((SEGS, SEGS), 0) == (at % RAYS_DEV) * 4 + at // RAYS_DEV)
    seg = dot(jnp.broadcast_to(seg_ref[...], (REGIONS, SEGS)).astype(F32).astype(BF16), order)
    region = iota((REGIONS, SEGS), 0).astype(F32)
    member = seg == region
    rank = dot(as_mask(member), as_mask(iota((SEGS, SEGS), 0) < at))
    slot = jnp.sum(jnp.where(member, rank + region * CAP, 0.0), axis=0, keepdims=True)
    onehot = as_mask(iota((SLOTS, SEGS), 0).astype(F32) == slot)
    parts = []
    for q in range(4):
        cut = slice(q * SEG_LEN, (q + 1) * SEG_LEN)
        parts.append(
            jnp.concatenate(
                [pos_ref[0, :, cut], pos_ref[1, :, cut], pos_ref[2, :, cut], sp_ref[:, cut]], axis=1
            )
        )
    data = jnp.concatenate(parts, axis=0)
    send_ref[...] = pick_left(onehot, data, NN)
    half = iota((8, 128), 1) // SEGS == parity
    ids = jnp.broadcast_to(jnp.concatenate([slot, slot], axis=1), (5, 128))
    spread = as_mask(iota((RAYS_DEV, 128), 1) % RAYS_DEV == iota((RAYS_DEV, 128), 0))
    tg = pick(jnp.concatenate([tg_ref[...], tg_ref[...], tg_ref[0:2, :]], axis=0), spread, NN)
    meta_ref[...] = jnp.where(half, jnp.concatenate([ids, tg[0:3]], axis=0), 0.0)


def dispatch(positions, spacing, targets, seg_region):
    return pl.pallas_call(
        dispatch_kernel,
        in_specs=[pl.BlockSpec(memory_space=pltpu.VMEM)] * 4,
        out_shape=(
            jax.ShapeDtypeStruct((SLOTS, 128), F32),
            pltpu.HBM((8, 128), F32),
        ),
        name="dispatch",
    )(positions, spacing, targets, seg_region)


def encode(pos, freq, first, count):
    cols = []
    for t in range(count):
        at = first + t
        cols.append(
            (freq[:, 0:1] * pos(0, at) + freq[:, 1:2] * pos(1, at)) + freq[:, 2:3] * pos(2, at)
        )
    turns = jnp.concatenate(cols, axis=1)
    x = turns - jnp.floor(turns + 0.5)
    y = x * x
    sine = x * (SIN[0] + y * (SIN[1] + y * (SIN[2] + y * (SIN[3] + y * SIN[4]))))
    cosine = COS[0] + y * (COS[1] + y * (COS[2] + y * (COS[3] + y * COS[4])))
    twice = sine + sine
    return jnp.concatenate([twice * cosine, 1.0 - twice * sine], axis=0).astype(BF16)


def local_render(raw, spacing):
    value = raw[0]
    small = jnp.exp(-jnp.abs(value))
    log1p = jnp.where(
        small < 0.02,
        small * (1.0 - small * (0.5 - small * (1.0 / 3.0 - small * 0.25))),
        jnp.log(1.0 + small),
    )
    density = jnp.maximum(value, 0.0) + log1p
    depth = density * spacing
    before = as_mask(iota((SEG_LEN, SEG_LEN), 1) < iota((SEG_LEN, SEG_LEN), 0))
    transmit = jnp.exp(-pick_left(before, depth, NN))
    fade = jnp.exp(-depth)
    opaque = jnp.where(
        depth < 0.03,
        depth * (1.0 - depth * (0.5 - depth * (1.0 / 6.0 - depth * (1.0 / 24.0)))),
        1.0 - fade,
    )
    weight = transmit * opaque
    tints = [0.5 + 0.5 * jnp.tanh(0.5 * raw[c]) for c in (1, 2, 3)]
    return depth, transmit, fade, weight, tints


def forward_kernel(
    recv_ref, meta_ref, freq_ref, win_ref, wh_ref, head_ref,
    send_ref, enc_ref, half_ref, local_ref,
    pos_ref, raw_ref, meta_copy, halves, encoded, local, send, sem, out_sem, *, chunk,
):
    meta = pltpu.make_async_copy(meta_ref, meta_copy, sem)
    meta.start()
    pos_ref[...] = jnp.transpose(recv_ref[...])
    count = chunk // SLOTS

    def pos(c, at):
        return pos_ref[c * SEG_LEN + at : c * SEG_LEN + at + 1, :]

    starts = range(0, ROWS, chunk)
    acts = []
    for start in starts:
        acts.append(encode(pos, freq_ref[...], start // SLOTS, count))
        encoded[:, start : start + chunk] = acts[-1]
    copies = [pltpu.make_async_copy(encoded, enc_ref, out_sem.at[LAYERS + 1])]
    copies[-1].start()
    for index in range(LAYERS + 1):
        weight = win_ref[...] if index == 0 else wh_ref[index - 1]
        for i, start in enumerate(starts):
            half = dot(weight, acts[i])
            acts[i] = (half + half * jnp.tanh(half)).astype(BF16)
            halves[index, :, start : start + chunk] = half.astype(BF16)
            if index == LAYERS:
                cut = pl.ds(start, chunk)
                at = out_sem.at[LAYERS + 3 + i] if i else out_sem.at[LAYERS]
                copies.append(pltpu.make_async_copy(halves.at[index, :, cut], half_ref.at[index, :, cut], at))
                copies[-1].start()
        if index < LAYERS:
            copies.append(pltpu.make_async_copy(halves.at[index], half_ref.at[index], out_sem.at[index]))
            copies[-1].start()
    for i, act in enumerate(acts):
        raw = dot(head_ref[...], act)
        for t in range(count):
            for c in range(4):
                raw_ref[c, i * count + t : i * count + t + 1, :] = raw[c : c + 1, t * SLOTS : (t + 1) * SLOTS]
    raw = [raw_ref[c] for c in range(4)]
    spacing = pos_ref[3 * SEG_LEN : 4 * SEG_LEN, :]
    depth, transmit, fade, weight, tints = local_render(raw, spacing)
    rows = [jnp.sum(depth, axis=0, keepdims=True)]
    rows += [jnp.sum(weight * tint, axis=0, keepdims=True) for tint in tints]
    meta.wait()
    block = jnp.concatenate(rows + [meta_copy[4:8, :]], axis=0)
    for r in range(REGIONS):
        send[r] = block
    copies.append(pltpu.make_async_copy(send, send_ref, out_sem.at[LAYERS + 3]))
    copies[-1].start()
    steep = (0.5 + 0.5 * jnp.tanh(0.5 * raw[0])) * spacing
    local[0] = transmit * fade * steep
    local[1] = steep
    for c in range(3):
        local[2 + c] = tints[c]
        local[5 + c] = weight * (tints[c] * (1.0 - tints[c]))
    local[8] = weight
    copies.append(pltpu.make_async_copy(local, local_ref, out_sem.at[LAYERS + 2]))
    copies[-1].start()
    for copy in copies:
        copy.wait()


def in_vmem(count):
    return [pl.BlockSpec(memory_space=pltpu.VMEM)] * count


def in_hbm(count):
    return [pl.BlockSpec(memory_space=pltpu.HBM)] * count


def forward_call(recv, meta, freq, win_t, wh_t, head, chunk=2048):
    kernel = lambda *refs: forward_kernel(*refs, chunk=chunk)
    specs = in_vmem(6)
    specs[1] = in_hbm(1)[0]
    meta = pltpu.with_memory_space_constraint(meta, pltpu.HBM)
    return pl.pallas_call(
        kernel,
        in_specs=specs,
        out_shape=(
            pltpu.HBM((REGIONS, 8, SLOTS), F32),
            pltpu.HBM((ENC, ROWS), BF16),
            pltpu.HBM((LAYERS + 1, HID, ROWS), BF16),
            pltpu.HBM((9, SEG_LEN, SLOTS), F32),
        ),
        out_specs=tuple(in_hbm(4)),
        scratch_shapes=[
            pltpu.VMEM((128, SLOTS), F32),
            pltpu.VMEM((4, SEG_LEN, SLOTS), F32),
            pltpu.VMEM((8, SLOTS), F32),
            pltpu.VMEM((LAYERS + 1, HID, ROWS), BF16),
            pltpu.VMEM((ENC, ROWS), BF16),
            pltpu.VMEM((9, SEG_LEN, SLOTS), F32),
            pltpu.VMEM((REGIONS, 8, SLOTS), F32),
            pltpu.SemaphoreType.DMA,
            pltpu.SemaphoreType.DMA((LAYERS + 3 + ROWS // chunk,)),
        ],
        compiler_params=pltpu.CompilerParams(vmem_limit_bytes=VMEM_LIMIT),
        cost_estimate=pl.CostEstimate(flops=2 * ROWS * 296000, bytes_accessed=700000, transcendentals=ROWS * 1280),
        name="forward",
    )(recv, meta, freq, win_t, wh_t, head)


def composite(me, got, gain):
    pairs = REGIONS // 2
    values = jnp.concatenate([got[r] for r in range(REGIONS)], axis=0)
    hi, mid, low = split3(values)
    lane = iota((1, 128), 1)
    sub = iota((128, 128), 0)
    depth_rows, colour_rows, target_rows, onehots = [], [[], [], []], [[], [], []], []
    for m in range(pairs):
        meta = got[2 * m, 4:8, :] + got[2 * m + 1, 4:8, :]
        ids = meta[0:1, :].astype(jnp.int32)
        owner = ids // CAP
        place = (2 * m + lane // SEGS) * CAP + ids % CAP
        onehot = sub == place
        picked = as_mask(onehot)
        found = dot(hi, picked) + (dot(mid, picked) + dot(low, picked))
        total = jnp.zeros((8, 128), F32)
        for r in range(REGIONS):
            total = total + jnp.where(owner == r, found[8 * r : 8 * r + 8], 0.0)
        depth_rows.append(total[0:1])
        for c in range(3):
            colour_rows[c].append(total[1 + c : 2 + c])
            target_rows[c].append(meta[1 + c : 2 + c])
        onehots.append(as_mask(jnp.logical_and(onehot, owner == me)))
    depth = jnp.concatenate(depth_rows, axis=0)
    colours = [jnp.concatenate(rows, axis=0) for rows in colour_rows]
    targets = [jnp.concatenate(rows, axis=0) for rows in target_rows]
    within = iota((pairs, 128), 1) % SEGS

    def earlier(x):
        total = jnp.zeros_like(x)
        for k in (1, 2, 3):
            total = total + jnp.where(within >= k * RAYS_DEV, pltpu.roll(x, k * RAYS_DEV, 1), 0.0)
        return total

    def later(x):
        total = jnp.zeros_like(x)
        for k in (1, 2, 3):
            total = total + jnp.where(within < SEGS - k * RAYS_DEV, pltpu.roll(x, 128 - k * RAYS_DEV, 1), 0.0)
        return total

    transmit = jnp.exp(-earlier(depth))
    behind = jnp.zeros((pairs, 128), F32)
    pixels, scaled = [], []
    for c in range(3):
        weighted = transmit * colours[c]
        after = later(weighted)
        pixel = (earlier(weighted) + weighted) + after
        pull = (pixel - targets[c]) * gain
        behind = behind + pull * after
        scaled.append(transmit * pull)
        pixels.append(pixel)
    rows = scaled + [behind]
    slots = jnp.zeros((32, SLOTS), F32)
    for m in range(pairs):
        x = jnp.concatenate([r[m : m + 1] for r in rows] + [jnp.zeros((4, 128), F32)], axis=0)
        parts = jnp.concatenate([p.astype(F32) for p in split3(x)] + [jnp.zeros((8, 128), F32)], axis=0)
        slots = slots + dot(parts.astype(BF16), onehots[m], NT)
    slots = slots[0:8] + (slots[8:16] + slots[16:24])
    own = []
    mine = jnp.logical_and(iota((pairs, 128), 0) == me // 2, iota((pairs, 128), 1) // SEGS == me % 2)
    for c in range(3):
        row = jnp.sum(jnp.where(mine, pixels[c], 0.0), axis=0, keepdims=True)
        own.append((row + pltpu.roll(row, SEGS, 1))[:, 0:RAYS_DEV])
    return slots, jnp.concatenate(own, axis=0)


def residual_of(half):
    tanh = jnp.tanh(half)
    above = 1.0 + tanh
    return half * above, above + half * (above * (1.0 - tanh))


def fetch_kernel(local_in, half_in, local_ref, top_ref, sem):
    copies = [
        pltpu.make_async_copy(half_in.at[LAYERS], top_ref, sem.at[0]),
        pltpu.make_async_copy(local_in, local_ref, sem.at[1]),
    ]
    for copy in copies:
        copy.start()
    for copy in copies:
        copy.wait()


def fetch_call(local, half):
    return pl.pallas_call(
        fetch_kernel,
        in_specs=in_hbm(2),
        out_specs=tuple(in_vmem(2)),
        out_shape=(
            jax.ShapeDtypeStruct((9, SEG_LEN, SLOTS), F32),
            jax.ShapeDtypeStruct((HID, ROWS), BF16),
        ),
        scratch_shapes=[pltpu.SemaphoreType.DMA((2,))],
        compiler_params=pltpu.CompilerParams(vmem_limit_bytes=16 * 1024 * 1024),
        cost_estimate=pl.CostEstimate(flops=2 * 10**9, bytes_accessed=2 * 10**7, transcendentals=0),
        name="fetch",
    )(*[pltpu.with_memory_space_constraint(x, pltpu.HBM) for x in (local, half)])


def backward_kernel(
    got_ref, wh_ref, head_ref, local_ref, top_ref, enc_in, half_in,
    pix_ref, keep_ref, send_ref, up_ref, gin_ref, gh_ref, halves, enc_ref, in_sem, *, chunk, gain,
):
    copies = [
        pltpu.make_async_copy(half_in.at[index], halves.at[index], in_sem.at[index]) for index in range(LAYERS)
    ]
    copies.append(pltpu.make_async_copy(enc_in, enc_ref, in_sem.at[LAYERS]))
    for copy in copies[LAYERS - 1 :: -1] + copies[LAYERS:]:
        copy.start()
    slots, pixel = composite(lax.axis_index("region"), got_ref, gain)
    pix_ref[...] = pixel
    pull = jnp.zeros((SEG_LEN, SLOTS), F32)
    for c in range(3):
        pull = pull + slots[c : c + 1] * local_ref[2 + c]
    after = as_mask(iota((SEG_LEN, SEG_LEN), 1) > iota((SEG_LEN, SEG_LEN), 0))
    rest = pick_left(after, local_ref[8] * pull, NN) + slots[3:4]
    ups = [local_ref[0] * pull - rest * local_ref[1]]
    ups += [slots[c : c + 1] * local_ref[5 + c] for c in range(3)]
    up_ref[...] = jnp.zeros_like(up_ref)
    for c in range(4):
        for t in range(SEG_LEN):
            up_ref[c : c + 1, t * SLOTS : (t + 1) * SLOTS] = ups[c][t : t + 1]

    cuts = [slice(start, start + chunk) for start in range(0, ROWS, chunk)]

    def residual(index, cut):
        half = top_ref[:, cut] if index == LAYERS else halves[index, :, cut]
        return residual_of(half)

    flows, slopes = [], []
    ghead = jnp.zeros((8, HID), F32)
    for cut in cuts:
        up = up_ref[:, cut].astype(BF16)
        flows.append(dot(head_ref[...], up))
        act, slope = residual(LAYERS, cut)
        slopes.append(slope)
        ghead = ghead + dot(up, act, NT)
    core = lax.axis_index("dp") % 2
    for index in range(LAYERS, -1, -1):
        for copy in {LAYERS: copies[LAYERS - 1 : LAYERS], LAYERS - 1: copies[1 : LAYERS - 1], 1: [copies[0], copies[LAYERS]]}.get(index, []):
            copy.wait()
        total = None
        for i, cut in enumerate(cuts):
            back = flows[i].astype(BF16) * slopes[i]
            if index > 0:
                flows[i] = dot(wh_ref[index - 1], back)
                act, slopes[i] = residual(index - 1, cut)
            else:
                act = enc_ref[:, cut]
            part = dot(act, back, NT)
            total = part if total is None else total + part
        if index > 0:
            gh_ref[index - 1] = total
        else:
            gin_ref[...] = total
        for ref, which in ((keep_ref, core), (send_ref, 1 - core)):
            for z in range(8):
                to = z * 2 + which
                if index > 0:
                    rows = gh_ref[index - 1, pl.ds(pl.multiple_of(to * 16, 16), 16), :]
                    ref[z, (index - 1) * 16 : index * 16, :] = rows.astype(BF16)
                else:
                    rows = gin_ref[pl.ds(pl.multiple_of(to * 8, 8), 8), :]
                    ref[z, 64:80, :] = jnp.concatenate([rows, ghead], axis=0).astype(BF16)


def backward_call(got, wh, head, local, top, enc, half, gain, chunk=512):
    enc, half = [pltpu.with_memory_space_constraint(x, pltpu.HBM) for x in (enc, half)]
    kernel = lambda *refs: backward_kernel(*refs, chunk=chunk, gain=gain)
    return pl.pallas_call(
        kernel,
        in_specs=in_vmem(5) + in_hbm(2),
        out_shape=(
            jax.ShapeDtypeStruct((3, RAYS_DEV), F32),
            jax.ShapeDtypeStruct((8, BLOCK, HID), BF16),
            jax.ShapeDtypeStruct((8, BLOCK, HID), BF16),
        ),
        scratch_shapes=[
            pltpu.VMEM((8, ROWS), F32),
            pltpu.VMEM((ENC, HID), F32),
            pltpu.VMEM((LAYERS, HID, HID), F32),
            pltpu.VMEM((LAYERS, HID, ROWS), BF16),
            pltpu.VMEM((ENC, ROWS), BF16),
            pltpu.SemaphoreType.DMA((LAYERS + 1,)),
        ],
        compiler_params=pltpu.CompilerParams(vmem_limit_bytes=BACK_LIMIT),
        cost_estimate=pl.CostEstimate(flops=4 * ROWS * 296000, bytes_accessed=23000000, transcendentals=0),
        name="backward",
    )(got, wh, head, local, top, enc, half)


def total_kernel(got_ref, gin_ref, gh_ref, ghead_ref):
    total = got_ref[0].astype(F32)
    for z in range(1, 8):
        total = total + got_ref[z].astype(F32)
    for l in range(LAYERS):
        gh_ref[0, l] = total[l * 16 : (l + 1) * 16]
    gin_ref[0] = total[64:72]
    mine = iota((HID, 16), 0) == lax.axis_index("dp") * 16 + iota((HID, 16), 1)
    ghead_ref[0] = pick(total[72:80], as_mask(mine), NN)[0:4]


def total_call(got):
    return pl.pallas_call(
        total_kernel,
        in_specs=in_vmem(1),
        out_shape=(
            jax.ShapeDtypeStruct((1, 8, HID), F32),
            jax.ShapeDtypeStruct((1, LAYERS, 16, HID), F32),
            jax.ShapeDtypeStruct((1, 4, 16), F32),
        ),
        name="total",
    )(got)


def per_device(positions, spacing, targets, frequencies, seg_region, w_in, w_hidden, w_head):
    rays = spacing.shape[0] * lax.axis_size("region") * lax.axis_size("dp")
    gain = LOSS_GAIN / math.sqrt(rays)

    half = jnp.asarray(0.5, BF16)
    win_t = w_in[0].T * half
    wh_t = jnp.transpose(w_hidden[0], (0, 2, 1)) * half
    wh_half = w_hidden[0] * half
    head = w_head[0]
    head_t = jnp.pad(head, ((0, 4), (0, 0))).T * half
    freq = frequencies.T

    outgoing, meta = dispatch(positions, spacing, targets, seg_region.reshape(1, SEGS))
    arrived = lax.all_to_all(
        outgoing.reshape(REGIONS, CAP, 128), "region", split_axis=0, concat_axis=0, tiled=True
    ).reshape(SLOTS, 128)
    summary, enc, half_pre, local = forward_call(arrived, meta, freq, win_t, wh_t, head)
    got = lax.all_to_all(summary, "region", split_axis=0, concat_axis=0, tiled=True)
    local, top = fetch_call(local, half_pre)
    pixel_color, keep, send = backward_call(got, wh_half, head_t, local, top, enc, half_pre, gain)
    other = lax.ppermute(send, "dp", [(i, i ^ 1) for i in range(16)])
    both = (keep.astype(F32) + other.astype(F32)).astype(BF16)
    groups = [list(range(0, 16, 2)), list(range(1, 16, 2))]
    parts = lax.all_to_all(both, "dp", 0, 0, tiled=True, axis_index_groups=groups)
    grad_in, grad_hidden, grad_head = total_call(parts)
    return pixel_color, grad_in, grad_hidden, grad_head


def solution(mesh):
    return jax.shard_map(
        per_device,
        mesh=mesh,
        in_specs=(
            P(None, ("region", "dp"), None),
            P(("region", "dp"), None),
            P(None, ("region", "dp")),
            P(),
            P(("region", "dp"), None),
            P("region", None, None),
            P("region", None, None, None),
            P("region", None, None),
        ),
        out_specs=(
            P(None, ("region", "dp")),
            P("region", "dp", None),
            P("region", None, "dp", None),
            P("region", None, "dp"),
        ),
        check_vma=False,
    )
```
